32 devices in a mesh: batch: 4 (over z), height: 2 (over core), chan: 4 (over y, x).
Axes of the slice: x: 2, y: 2, z: 4, core: 2. Of those that a mesh axis runs over, the one named last changes fastest.
Arguments:
- features: bfloat16 [8, 8, 64, 640], P('height', None, 'batch', 'chan'), may hold values from -6 to 6
- gains: float32 [2, 640], P(None, 'chan'), may hold values from 0.25 to 1.75
- biases: float32 [2, 640], P(None, 'chan'), may hold values from -3 to 3
- conv_one: bfloat16 [640, 3, 3, 640], P('chan'), may hold values from -0.078125 to 0.078125
- conv_two: bfloat16 [640, 3, 3, 640], P('chan'), may hold values from -0.078125 to 0.078125
- out_grad: bfloat16 [8, 8, 64, 640], P('height', None, 'batch', 'chan'), may hold values from -6 to 6
- counts: int32 [4], replicated, may hold values from 4 to 16, as said below
- running_prior: float32 [4, 640], P(None, 'chan'), may hold values from 0.5 to 2
- momentum: float32 [1], replicated, may hold values from 0.05 to 0.5
Outputs:
- output: bfloat16 [8, 8, 64, 640], P('height', None, 'batch', 'chan')
- input_grad: bfloat16 [8, 8, 64, 640], P('height', None, 'batch', 'chan')
- conv_one_grad: float32 [640, 3, 3, 640], P('chan')
- conv_two_grad: float32 [640, 3, 3, 640], P('chan')
- norm_grads: float32 [4, 640], P(None, 'chan')
- running_stats: float32 [4, 640], P(None, 'chan')
The draws below stay inside these ranges and needn't reach their ends.
Inputs may be any that keep to these rules, and one draw needn't show every extreme that they name: Entry b counts the valid images among the 16 slots at index b of batch; they are that index's first slots, the others padding. Some entry equals 16.
All inputs are finite; a program needn't handle non-finite values.
Results may differ from the reference program's by a relative error of at most 0.0063.
Values may be sent and summed in bfloat16 or wider, within the bound.
A program may use at most 64 MiB of HBM per device.

```python
import jax
import jax.numpy as jnp
from jax import lax

C = 640
SIDE = 8
IMG_DEV = 16
IMAGES = 64
N_BATCH = 4


def draw_counts(key, part):
    key = jax.random.fold_in(key, 11)
    base_counts = jax.random.randint(key, (N_BATCH,), IMG_DEV // 4, IMG_DEV + 1)
    chosen = jax.random.randint(jax.random.fold_in(key, 5), (), 0, N_BATCH)
    return jnp.where(jnp.arange(N_BATCH) == chosen, IMG_DEV, base_counts).astype(jnp.int32)


def block_scale(key, shape, cuts, low, high):
    level, own = 1.0, jax.random.fold_in(key, 6)
    for dim, shards_of in cuts:
        heights = jnp.exp(jax.random.uniform(jax.random.fold_in(own, dim), (shards_of,), jnp.float32, low / len(cuts), high / len(cuts)))
        level = level * jnp.repeat(heights, shape[dim] // shards_of).reshape([-1 if axis == dim else 1 for axis in range(len(shape))])
    return level


def scatter_about(rng, extent, deviation, limit, pieces=(), kind=jnp.bfloat16):
    drawn = jax.random.normal(rng, extent, jnp.float32) * deviation
    if len(pieces) > 0:
        drawn = block_scale(rng, extent, pieces, -0.22, 0.18) * drawn
    return jnp.clip(drawn, min=-limit, max=limit).astype(kind)


def setup_inputs(seed: int = 0) -> dict:
    splits = jax.random.split(jax.random.key(seed), 10)
    features = scatter_about(splits[0], (SIDE, SIDE, IMAGES, C), 1.0, 6.0, ((0, 2), (2, 4), (3, 4)))
    gains = jnp.clip(1.0 + 0.15 * jax.random.normal(splits[1], (2, C), jnp.float32), 0.25, 1.75)
    biases = scatter_about(splits[2], (2, C), 0.5, 3.0, ((1, 4),), jnp.float32)
    conv_one = scatter_about(splits[3], (C, 3, 3, C), (9 * C) ** -0.5, 0.078125, ((0, 4),))
    conv_two = scatter_about(splits[4], (C, 3, 3, C), (9 * C) ** -0.5, 0.078125, ((0, 4),))
    out_grad = scatter_about(splits[5], (SIDE, SIDE, IMAGES, C), 1.0, 6.0, ((0, 2), (2, 4), (3, 4)))
    counts = draw_counts(jax.random.fold_in(splits[9], 71), 0)
    running_prior = jnp.clip(0.5 + 1.5 * jax.random.uniform(splits[7], (4, C), jnp.float32) ** block_scale(splits[7], (4, C), ((1, 4),), -0.2, 0.2), 0.5, 2.0)
    momentum = jnp.clip(jax.random.uniform(splits[8], (1,), jnp.float32, 0.05, 0.5), 0.05, 0.5)
    return dict(features=features, gains=gains, biases=biases, conv_one=conv_one, conv_two=conv_two, out_grad=out_grad, counts=counts, running_prior=running_prior, momentum=momentum)


@jax.custom_vjp
def low(v):
    return lax.optimization_barrier(v.astype(jnp.bfloat16)).astype(jnp.float32)

@jax.custom_vjp
def low_back(v):
    return v

def low_keep(v):
    return (low(v), None)

def low_pass(kept, grad):
    return (grad,)

def back_keep(v):
    return (v, None)

def back_low(kept, grad):
    return (low(grad),)
low.defvjp(low_keep, low_pass)
low_back.defvjp(back_keep, back_low)
epsilon = 1e-05

def convolve(acts, weights):
    return lax.conv_general_dilated(acts, weights, (1, 1), ((1, 1), (1, 1)), dimension_numbers=('HWNC', 'OHWI', 'HWNC'), precision=lax.Precision.HIGHEST)

def normalize(values, gain, bias, valid_mask, pixel_total):
    mean_vec = lax.optimization_barrier(jnp.sum(valid_mask * values, axis=(0, 1, 2))) / pixel_total
    centered = values - mean_vec
    var_vec = lax.optimization_barrier(jnp.sum(valid_mask * centered * centered, axis=(0, 1, 2))) / pixel_total
    scaled = centered * lax.rsqrt(var_vec + epsilon)
    return (gain * scaled + bias, mean_vec, var_vec)

def reference(features, gains, biases, conv_one, conv_two, out_grad, counts, running_prior, momentum):
    slot_index = jnp.arange(IMAGES, dtype=jnp.int32)
    owner = (slot_index // IMG_DEV).astype(jnp.int32)
    valid_flat = (slot_index % IMG_DEV < counts[owner]).astype(jnp.float32)
    valid_mask = valid_flat.reshape(1, 1, IMAGES, 1)
    pixel_total = jnp.sum(valid_flat) * (SIDE * SIDE)

    def forward(xf, gain_rows, bias_rows, first, second):
        pre_one, mean_one, var_one = normalize(xf, gain_rows[0], bias_rows[0], valid_mask, pixel_total)
        act_one = low(jax.nn.silu(pre_one))
        middle = low_back(convolve(act_one, first))
        pre_two, mean_two, var_two = normalize(middle, gain_rows[1], bias_rows[1], valid_mask, pixel_total)
        act_two = low(jax.nn.silu(pre_two))
        branch = low_back(convolve(act_two, second))
        return ((xf + branch) * valid_mask, jnp.stack([mean_one, var_one, mean_two, var_two]))
    primal, pullback, batch_stats = jax.vjp(forward, features.astype(jnp.float32), gains, biases, conv_one.astype(jnp.float32), conv_two.astype(jnp.float32), has_aux=True)
    grad_x, grad_gains, grad_biases, grad_first, grad_second = pullback(out_grad.astype(jnp.float32))
    unbias = pixel_total / (pixel_total - 1.0)
    one_value = jnp.ones((), jnp.float32)
    row_scale = jnp.stack([one_value, unbias, one_value, unbias])
    rate = momentum[0]
    running_stats = (1.0 - rate) * running_prior + rate * batch_stats * row_scale[:, None]
    norm_grads = jnp.stack([grad_gains[0], grad_biases[0], grad_gains[1], grad_biases[1]])
    return (primal.astype(jnp.bfloat16), grad_x.astype(jnp.bfloat16), grad_first, grad_second, norm_grads, running_stats)
```

```python
import functools

import jax
import jax.numpy as jnp
from jax import lax
from jax.experimental import pallas as pl
from jax.experimental.pallas import tpu as pltpu
from jax.sharding import PartitionSpec as P

MESH = pl.DeviceIdType.MESH
EPSILON = 1e-05
F32 = jnp.float32
BF16 = jnp.bfloat16

CHAN = 4
ROWS = 4
COLS = 8
IMG = 16
LINE = COLS * IMG
PIX = ROWS * LINE
WIDE = LINE + 2 * IMG
OWN = 160
FULL = CHAN * OWN
LANES = 128
TAIL = OWN - LANES
PACK = PIX + LINE
HALF = OWN // 2
TAPS = 9
CHUNKS = 2 * TAPS
SKEW = 3
KINDS = 4


def dot(a, b, contract):
    return lax.dot_general(a, b, ((contract), ((), ())), preferred_element_type=F32)


def turn(x, shift):
    shift = shift % LANES
    return x if shift == 0 else pltpu.roll(x, shift, 1)


def lane_ids(rows):
    return lax.broadcasted_iota(jnp.int32, (rows, LANES), 1)


def pack_tails(tails):
    group = lane_ids(LINE) // TAIL
    packed = tails[0]
    for row in range(1, ROWS):
        packed = jnp.where(group == row, turn(tails[row], TAIL * row), packed)
    return packed


def merge_row(blocks, row):
    lane = lane_ids(LINE)
    main = [b[pl.ds(LINE * row, LINE), :].astype(F32) for b in blocks]
    tail = [b[pl.ds(PIX, LINE), :].astype(F32) for b in blocks]
    one, two, three = turn(main[1], 32), turn(main[2], 64), turn(main[3], 96)

    def moved(k, to):
        return turn(tail[k], to - TAIL * row)

    return [
        main[0],
        jnp.where(lane < 32, moved(0, 0), one),
        jnp.where(lane < 32, one, jnp.where(lane < 64, moved(1, 32), two)),
        jnp.where(lane < 64, two, jnp.where(lane < 96, moved(2, 64), three)),
        jnp.where(lane < 96, three, moved(3, 96)),
    ]


def split_row(pieces):
    lane = lane_ids(LINE)
    p0, p1, p2, p3, p4 = pieces
    mains = [
        p0,
        jnp.where(lane < 96, turn(p1, -32), turn(p2, -32)),
        jnp.where(lane < 64, turn(p2, -64), turn(p3, -64)),
        jnp.where(lane < 32, turn(p3, 32), turn(p4, 32)),
    ]
    tails = [p1, turn(p2, -32), turn(p3, -64), turn(p4, -96)]
    return mains, tails


def block_kernel(
    nb,
    x_ref, dy_ref, gains_ref, biases_ref, prior_ref, counts_ref, rate_ref, w1_hbm, w2_hbm,
    out_ref, din_ref, dw_hbm, ng_ref, rs_ref,
    w1, w2, xf, mid, acc, wide_acc, gact, gpre, par, a1, a2, g2, gm, gt,
    stats0, stats1, stats2, stats3, gat0, gat1, red0, red1, red_send, own_red, d2d_out, d2d_in, part, z_in, z_out, dw_ref,
    w_sem, st_send, st_recv, ga_send, ga_recv, ha_send, ha_recv,
    d2_send, d2_recv, z_send, z_recv, fz_send, fz_recv, fd_send, fd_recv, dw_sem,
):
    b = lax.axis_index("batch")
    h = lax.axis_index("height")
    c = lax.axis_index("chan")
    group = 2 * nb
    me = 2 * b + h
    stats, gat, red = (stats0, stats1, stats2, stats3), (gat0, gat1), (red0, red1)

    def remote(src, dst, send, recv, to):
        return pltpu.make_async_remote_copy(
            src_ref=src, dst_ref=dst, send_sem=send, recv_sem=recv, device_id=to, device_id_type=MESH
        )

    def at_group(j):
        return (lax.div(j, 2), lax.rem(j, 2), c)

    def at_chan(k):
        return (b, h, k)

    core = (b, 1 - h, c)

    loads = [
        pltpu.make_async_copy(w2_hbm, w2, w_sem.at[1]),
        pltpu.make_async_copy(w1_hbm, w1, w_sem.at[0]),
    ]
    for load in loads:
        load.start()

    barrier = pltpu.get_barrier_semaphore()

    @pl.loop(1, group)
    def _(d):
        pl.semaphore_signal(barrier, inc=1, device_id=at_group(lax.rem(me + d, group)), device_id_type=MESH)

    @pl.loop(1, CHAN)
    def _(d):
        pl.semaphore_signal(barrier, inc=1, device_id=at_chan(lax.rem(c + d, CHAN)), device_id_type=MESH)

    count = counts_ref[b]
    valid = (lax.broadcasted_iota(jnp.int32, (LINE, 2 * LANES), 0) % IMG < count).astype(F32)
    total_images = lax.fori_loop(0, nb, lambda i, s: s + counts_ref[i], jnp.int32(0))
    total = (total_images * (COLS * COLS)).astype(F32)
    total_row = jnp.full((1, 2 * LANES), total, F32)

    par[...] = jnp.zeros_like(par)
    par[0:2, 0:OWN] = gains_ref[...]
    par[2:4, 0:OWN] = biases_ref[...]

    def line(row):
        return pl.ds(LINE * row, LINE)

    def column_sum(v):
        return jnp.sum(v, axis=0, keepdims=True)

    def local_stats(src, e):
        here = jnp.full((1, 2 * LANES), count * (ROWS * COLS), jnp.int32).astype(F32)
        s = jnp.zeros((1, 2 * LANES), F32)
        for row in range(ROWS):
            s += column_sum(valid * src[line(row), :])
        mean = s / here
        m2 = jnp.zeros((1, 2 * LANES), F32)
        for row in range(ROWS):
            d = src[line(row), :] - mean
            m2 += column_sum(valid * d * d)
        stats[e][me, 0:1, :] = s
        stats[e][me, 1:2, :] = m2

    def share_stats(e):
        @pl.loop(1, group)
        def _(d):
            remote(
                stats[e].at[me], stats[e].at[me], st_send.at[e, d], st_recv.at[e, me],
                at_group(lax.rem(me + d, group)),
            ).start()

    def stats_copy(e, d):
        j = lax.rem(me + d, group)
        return remote(stats[e].at[j], stats[e].at[j], st_send.at[e, d], st_recv.at[e, j], at_group(j))

    def await_stats(e):
        @pl.loop(1, group)
        def _(d):
            stats_copy(e, d).wait_recv()

    def sum_stats(e):
        return lax.fori_loop(0, group, lambda j, s: s + stats[e][j], jnp.zeros((8, 2 * LANES), F32))

    def norm_stats(e):
        tot = sum_stats(e)
        mean = tot[0:1] / total_row

        def spread(j, s):
            n = jnp.full((1, 2 * LANES), counts_ref[lax.div(j, 2)] * (ROWS * COLS), jnp.int32).astype(F32)
            d = stats[e][j][0:1] / n - mean
            return s + n * d * d

        var = (tot[1:2] + lax.fori_loop(0, group, spread, jnp.zeros((1, 2 * LANES), F32))) / total_row
        return mean, var

    def share_block(e, block_of, slot):
        @pl.loop(1, CHAN)
        def _(d):
            k = lax.rem(c + d, CHAN)
            remote(block_of(k), slot, ga_send.at[e, d], ga_recv.at[e, c], at_chan(k)).start()

    def await_block(e, buf):
        @pl.loop(1, CHAN)
        def _(d):
            k = lax.rem(c + d, CHAN)
            remote(buf.at[k], buf.at[k], ga_send.at[e, d], ga_recv.at[e, k], at_chan(k)).wait_recv()

    def edge_copy(e, buf):
        return remote(buf.at[ROWS - (ROWS - 1) * h], buf.at[(ROWS + 1) * h], ha_send.at[e], ha_recv.at[e], core)

    def edge_wait(e, buf):
        far = buf.at[(ROWS + 1) * (1 - h)]
        remote(far, far, ha_send.at[e], ha_recv.at[e], core).wait_recv()

    def clear_borders(buf):
        lanes = buf.shape[2]
        for row in range(1, ROWS + 1):
            buf[row, 0:IMG, :] = jnp.zeros((IMG, lanes), BF16)
            buf[row, IMG + LINE : WIDE, :] = jnp.zeros((IMG, lanes), BF16)
        buf[(ROWS + 1) * h] = jnp.zeros((WIDE, lanes), BF16)

    def window(buf, i, j):
        return buf[pl.ds(i, ROWS), pl.ds(pl.multiple_of(IMG * j, IMG), LINE), :].reshape(PIX, buf.shape[2])

    def conv_taps(i, src, weights):
        @pl.loop(0, 3)
        def _(j):
            acc[:, 0:OWN] += dot(window(src, i, j), weights[3 * i + j], ((1,), (1,)))

    def conv(src, weights, edge):
        acc[...] = jnp.zeros_like(acc)
        conv_taps(1, src, weights)
        if edge is not None:
            edge_wait(edge, src)
        conv_taps(0, src, weights)
        conv_taps(2, src, weights)

    def conv_back_taps(i, src, weights):
        @pl.loop(0, 3)
        def _(j):
            wide_acc[...] += dot(window(src, 2 - i, 2 - j), weights[3 * i + j], ((1,), (0,)))

    def conv_back(src, weights, edge, e):
        wide_acc[...] = jnp.zeros_like(wide_acc)
        conv_back_taps(1, src, weights)
        edge_wait(edge, src)
        conv_back_taps(0, src, weights)
        conv_back_taps(2, src, weights)
        tails = [[], [], [], []]
        for row in range(ROWS):
            pieces = [wide_acc[line(row), LANES * t : LANES * (t + 1)] for t in range(5)]
            mains, ends = split_row(pieces)
            for k in range(CHAN):
                own_red[k, line(row), :] = mains[k]
                tails[k].append(ends[k])
        for k in range(CHAN):
            own_red[k, PIX:PACK, :] = pack_tails(tails[k])

        @pl.loop(0, CHAN)
        def _(k):
            red_send[e - 2, k] = own_red[k].astype(BF16)

        share_block(e, lambda k: red_send.at[e - 2, k], red[e - 2].at[c])

    def gather_sum(e):
        await_block(e, red[e - 2])

        def add(d, s):
            return s + red[e - 2][lax.rem(c + d, CHAN)].astype(F32)

        packed = lax.fori_loop(1, CHAN, add, own_red[c])
        lane = lane_ids(LINE)
        tail = packed[PIX:PACK]
        for row in range(ROWS):
            gact[line(row), 0:LANES] = packed[LINE * row : LINE * (row + 1)]
            gact[line(row), LANES : 2 * LANES] = jnp.where(lane < TAIL, turn(tail, -TAIL * row), 0.0)

    def activate(src, mean, inv, gain, bias, e):
        tails = []
        for row in range(ROWS):
            pre = gain * ((src[line(row), :] - mean) * inv) + bias
            act = pre * jax.nn.sigmoid(pre)
            gat[e][c, line(row), :] = act[:, 0:LANES].astype(BF16)
            tails.append(act[:, LANES : 2 * LANES])
        gat[e][c, PIX:PACK, :] = pack_tails(tails).astype(BF16)
        share_block(e, lambda k: gat[e].at[c], gat[e].at[c])

    def spread_out(e, dst, edge):
        await_block(e, gat[e])
        blocks = [gat[e].at[k] for k in range(CHAN)]
        for row in range(ROWS):
            for t, piece in enumerate(merge_row(blocks, row)):
                dst[1 + row, IMG : IMG + LINE, LANES * t : LANES * (t + 1)] = piece.astype(BF16)
        edge_copy(edge, dst).start()

    def back_sums(src, mean, inv, gain, bias, e):
        s_gain = jnp.zeros((1, 2 * LANES), F32)
        s_bias = jnp.zeros((1, 2 * LANES), F32)
        for row in range(ROWS):
            hat = (src[line(row), :] - mean) * inv
            pre = gain * hat + bias
            sig = jax.nn.sigmoid(pre)
            grad = gact[line(row), :] * (sig * (1.0 + pre * (1.0 - sig)))
            gpre[line(row), :] = grad
            s_gain += column_sum(valid * grad * hat)
            s_bias += column_sum(valid * grad)
        stats[e][me, 0:1, :] = s_gain
        stats[e][me, 1:2, :] = s_bias
        share_stats(e)

    def filter_turn(src):
        for row in range(ROWS):
            own = src[1 + row, IMG : IMG + LINE, :].astype(F32)
            flipped = own.T.astype(BF16)
            gt[0, :, line(row)] = flipped
        gt[1, 0:HALF, :] = gt[0, pl.ds(pl.multiple_of(HALF * h, 16), HALF), :]
        gt[1, HALF:OWN, :] = gt[0, pl.ds(pl.multiple_of(HALF * (1 - h), 16), HALF), :]

    def filter_grad(base, src):
        @pl.loop(0, TAPS)
        def _(t):
            i, j = lax.div(t, 3), lax.rem(t, 3)
            r = dot(gt[1], window(src, i, j), ((1,), (0,)))
            part[base + t] = r[0:HALF]
            d2d_out[base + t] = r[HALF:OWN].astype(BF16)
            remote(
                d2d_out.at[base + t], d2d_in.at[base + t], d2_send.at[base + t], d2_recv.at[base + t], core
            ).start()

    middle = nb // 2
    left = b < middle
    is_end = jnp.logical_or(b == 0, b == nb - 1)
    is_mid = jnp.logical_or(b == middle - 1, b == middle)
    inner = (jnp.where(left, b + 1, b - 1), h, c)
    outer = (jnp.where(left, b - 1, b + 1), h, c)
    mid_off = jnp.where(is_mid, CHUNKS, 0)
    mine = pl.ds(pl.multiple_of(HALF * h, 16), HALF)
    yours = pl.ds(pl.multiple_of(HALF * (1 - h), 16), HALF)

    def inward(t):
        return remote(z_out.at[t], z_in.at[t + mid_off], z_send.at[t], z_recv.at[t + mid_off], inner)

    def outward(t):
        return remote(dw_ref.at[t, mine], dw_ref.at[t, mine], fz_send.at[t], fz_recv.at[t], outer)

    def across(t):
        return remote(dw_ref.at[t, mine], dw_ref.at[t, mine], fd_send.at[t], fd_recv.at[t], core)

    def store(t):
        return pltpu.make_async_copy(dw_ref.at[t], dw_hbm.at[t], dw_sem.at[t])

    def take_halves(base):
        @pl.loop(base, base + TAPS)
        def _(t):
            remote(d2d_out.at[t], d2d_in.at[t], d2_send.at[t], d2_recv.at[t], core).wait_recv()
            s = part[t] + d2d_in[t].astype(F32)

            @pl.when(is_end)
            def _():
                z_out[t] = s.astype(BF16)
                inward(t).start()

            @pl.when(jnp.logical_not(is_end))
            def _():
                part[t] = s

    def line_step(t):
        @pl.when(jnp.logical_and(t < CHUNKS, jnp.logical_not(is_end)))
        def _():
            remote(z_in.at[t], z_in.at[t], z_send.at[t], z_recv.at[t], outer).wait_recv()
            z_out[t] = (part[t] + z_in[t].astype(F32)).astype(BF16)
            inward(t).start()

        u = t - SKEW

        @pl.when(jnp.logical_and(t >= SKEW, u < CHUNKS))
        def _():
            @pl.when(is_mid)
            def _():
                remote(
                    z_in.at[CHUNKS + u], z_in.at[CHUNKS + u], z_send.at[u], z_recv.at[CHUNKS + u], inner
                ).wait_recv()
                dw_ref[u, mine, :] = (z_out[u].astype(F32) + z_in[CHUNKS + u].astype(F32)).astype(BF16)

            @pl.when(jnp.logical_not(is_mid))
            def _():
                remote(dw_ref.at[u, mine], dw_ref.at[u, mine], fz_send.at[u], fz_recv.at[u], inner).wait_recv()

            @pl.when(jnp.logical_not(is_end))
            def _():
                outward(u).start()

            across(u).start()

        v = u - 1

        @pl.when(v >= 0)
        def _():
            remote(dw_ref.at[v, yours], dw_ref.at[v, yours], fd_send.at[v], fd_recv.at[v], core).wait_recv()
            store(v).start()

    def line_steps(first, last):
        pl.loop(first, last)(line_step)

    xf[:, LANES : 2 * LANES] = jnp.zeros((PIX, LANES), F32)
    xf[:, 0:OWN] = x_ref[...].astype(F32)
    local_stats(xf, 0)
    for buf in (g2, a1, gm, a2):
        clear_borders(buf)
    for row in range(ROWS):
        g2[1 + row, IMG : IMG + LINE, :] = (dy_ref[line(row), :].astype(F32) * valid[:, 0:OWN]).astype(BF16)

    pl.semaphore_wait(barrier, group - 1 + CHAN - 1)
    share_stats(0)
    edge_copy(0, g2).start()

    loads[0].wait()
    conv_back(g2, w2, 0, 2)

    gain1, gain2, bias1, bias2 = (par[k : k + 1, :] for k in range(4))
    await_stats(0)
    mean1, var1 = norm_stats(0)
    inv1 = lax.rsqrt(var1 + EPSILON)
    activate(xf, mean1, inv1, gain1, bias1, 0)
    loads[1].wait()
    spread_out(0, a1, 1)
    conv(a1, w1, 1)
    mid[...] = acc[...]

    local_stats(mid, 1)
    share_stats(1)
    gather_sum(2)
    await_stats(1)
    mean2, var2 = norm_stats(1)
    inv2 = lax.rsqrt(var2 + EPSILON)
    activate(mid, mean2, inv2, gain2, bias2, 1)
    back_sums(mid, mean2, inv2, gain2, bias2, 2)
    await_stats(2)
    sums2 = sum_stats(2)

    scale2 = gain2 * inv2
    for row in range(ROWS):
        hat = (mid[line(row), :] - mean2) * inv2
        grad = valid * scale2 * (gpre[line(row), :] - sums2[1:2] / total_row - hat * (sums2[0:1] / total_row))
        gm[1 + row, IMG : IMG + LINE, :] = grad[:, 0:OWN].astype(BF16)
    edge_copy(2, gm).start()
    filter_turn(gm)
    filter_grad(0, a1)
    take_halves(0)

    spread_out(1, a2, 3)
    conv_back(gm, w1, 2, 3)
    filter_turn(g2)
    edge_wait(3, a2)
    filter_grad(TAPS, a2)
    take_halves(TAPS)

    line_steps(0, 4)
    conv(a2, w2, None)
    for row in range(ROWS):
        kept = (xf[line(row), :] + acc[line(row), :]) * valid
        out_ref[line(row), :] = kept[:, 0:OWN].astype(BF16)
    line_steps(4, 8)
    gather_sum(3)
    back_sums(xf, mean1, inv1, gain1, bias1, 3)
    line_steps(8, 12)
    await_stats(3)
    sums1 = sum_stats(3)
    scale1 = gain1 * inv1
    for row in range(ROWS):
        hat = (xf[line(row), :] - mean1) * inv1
        grad = valid * scale1 * (gpre[line(row), :] - sums1[1:2] / total_row - hat * (sums1[0:1] / total_row))
        din_ref[line(row), :] = (dy_ref[line(row), :].astype(F32) * valid[:, 0:OWN] + grad[:, 0:OWN]).astype(BF16)

    ng_ref[0:2, :] = sums1[0:2, 0:OWN]
    ng_ref[2:4, :] = sums2[0:2, 0:OWN]
    unbias = total_row / (total_row - 1.0)
    rate = rate_ref[0]
    for k, stat in enumerate((mean1, var1 * unbias, mean2, var2 * unbias)):
        rs_ref[k : k + 1, :] = (1.0 - rate) * prior_ref[k : k + 1, :] + rate * stat[:, 0:OWN]
    line_steps(12, CHUNKS + SKEW + 1)

    @pl.loop(0, CHUNKS)
    def _(t):
        store(t).wait()
        across(t).wait_send()
        inward(t).wait_send()
        remote(d2d_out.at[t], d2d_in.at[t], d2_send.at[t], d2_recv.at[t], core).wait_send()

        @pl.when(jnp.logical_not(is_end))
        def _():
            outward(t).wait_send()

    for e, buf in enumerate((g2, a1, gm, a2)):
        edge_copy(e, buf).wait_send()
    for e in range(KINDS):

        @pl.loop(1, group)
        def _(d):
            stats_copy(e, d).wait_send()

        @pl.loop(1, CHAN)
        def _(d):
            slot = gat[e].at[c] if e < 2 else red[e - 2].at[c]
            remote(slot, slot, ga_send.at[e, d], ga_recv.at[e, c], at_chan(lax.rem(c + d, CHAN))).wait_send()


def shards(features, gains, biases, conv_one, conv_two, out_grad, counts, running_prior, momentum):
    nb = lax.axis_size("batch")
    group = 2 * nb
    vmem, smem, hbm = (pl.BlockSpec(memory_space=s) for s in (pltpu.VMEM, pltpu.SMEM, pl.ANY))
    dma = pltpu.SemaphoreType.DMA
    out, din, dw, ng, rs = pl.pallas_call(
        functools.partial(block_kernel, nb),
        out_shape=(
            jax.ShapeDtypeStruct((PIX, OWN), BF16),
            jax.ShapeDtypeStruct((PIX, OWN), BF16),
            jax.ShapeDtypeStruct((CHUNKS, OWN, FULL), BF16),
            jax.ShapeDtypeStruct((4, OWN), F32),
            jax.ShapeDtypeStruct((4, OWN), F32),
        ),
        in_specs=[vmem, vmem, vmem, vmem, vmem, smem, smem, hbm, hbm],
        out_specs=(vmem, vmem, hbm, vmem, vmem),
        scratch_shapes=[
            pltpu.VMEM((TAPS, OWN, FULL), BF16),
            pltpu.VMEM((TAPS, OWN, FULL), BF16),
            pltpu.VMEM((PIX, 2 * LANES), F32),
            pltpu.VMEM((PIX, 2 * LANES), F32),
            pltpu.VMEM((PIX, 2 * LANES), F32),
            pltpu.VMEM((PIX, FULL), F32),
            pltpu.VMEM((PIX, 2 * LANES), F32),
            pltpu.VMEM((PIX, 2 * LANES), F32),
            pltpu.VMEM((8, 2 * LANES), F32),
            pltpu.VMEM((ROWS + 2, WIDE, FULL), BF16),
            pltpu.VMEM((ROWS + 2, WIDE, FULL), BF16),
            pltpu.VMEM((ROWS + 2, WIDE, OWN), BF16),
            pltpu.VMEM((ROWS + 2, WIDE, OWN), BF16),
            pltpu.VMEM((2, OWN, PIX), BF16),
            *[pltpu.VMEM((group, 8, 2 * LANES), F32)] * 4,
            *[pltpu.VMEM((CHAN, PACK, LANES), BF16)] * 2,
            *[pltpu.VMEM((CHAN, PACK, LANES), BF16)] * 2,
            pltpu.VMEM((2, CHAN, PACK, LANES), BF16),
            pltpu.VMEM((CHAN, PACK, LANES), F32),
            pltpu.VMEM((CHUNKS, HALF, FULL), BF16),
            pltpu.VMEM((CHUNKS, HALF, FULL), BF16),
            pltpu.VMEM((CHUNKS, HALF, FULL), F32),
            pltpu.VMEM((2 * CHUNKS, HALF, FULL), BF16),
            pltpu.VMEM((CHUNKS, HALF, FULL), BF16),
            pltpu.VMEM((CHUNKS, OWN, FULL), BF16),
            dma((2,)),
            dma((4, group)),
            dma((4, group)),
            dma((KINDS, CHAN)),
            dma((KINDS, CHAN)),
            dma((4,)),
            dma((4,)),
            dma((CHUNKS,)),
            dma((CHUNKS,)),
            dma((CHUNKS,)),
            dma((2 * CHUNKS,)),
            dma((CHUNKS,)),
            dma((CHUNKS,)),
            dma((CHUNKS,)),
            dma((CHUNKS,)),
            dma((CHUNKS,)),
        ],
        compiler_params=pltpu.CompilerParams(
            collective_id=0, has_side_effects=True, vmem_limit_bytes=48 * 1024 * 1024
        ),
    )(
        features.reshape(PIX, OWN),
        out_grad.reshape(PIX, OWN),
        gains,
        biases,
        running_prior,
        counts,
        momentum,
        jnp.transpose(conv_one, (1, 2, 0, 3)).reshape(TAPS, OWN, FULL),
        jnp.transpose(conv_two, (1, 2, 0, 3)).reshape(TAPS, OWN, FULL),
    )
    maps = (ROWS, COLS, IMG, OWN)

    def filters(first):
        taps = dw[first : first + TAPS].reshape(3, 3, OWN, FULL)
        return jnp.transpose(taps, (2, 0, 1, 3)).astype(F32)

    return (out.reshape(maps), din.reshape(maps), filters(0), filters(TAPS), ng, rs)


def solution(mesh):
    maps = P("height", None, "batch", "chan")
    rows = P(None, "chan")
    filters = P("chan", None, None, None)
    return jax.shard_map(
        shards,
        mesh=mesh,
        in_specs=(maps, rows, rows, filters, filters, maps, P(), rows, P()),
        out_specs=(maps, maps, filters, filters, rows, rows),
        check_vma=False,
    )
```

```python
import functools

import jax
import jax.numpy as jnp
from jax import lax
from jax.experimental import pallas as pl
from jax.experimental.pallas import tpu as pltpu
from jax.sharding import PartitionSpec as P

MESH = pl.DeviceIdType.MESH
EPSILON = 1e-05
F32 = jnp.float32
BF16 = jnp.bfloat16

CHAN = 4
ROWS = 4
COLS = 8
IMG = 16
LINE = COLS * IMG
PIX = ROWS * LINE
WIDE = LINE + 2 * IMG
OWN = 160
FULL = CHAN * OWN
LANES = 128
TAIL = OWN - LANES
PACK = PIX + LINE
HALF = OWN // 2
TAPS = 9
CHUNKS = 2 * TAPS
FLAT = TAPS * HALF
STEP = 48
THREE = 3 * HALF
SKEW = 3
FAR_SKEW = 6
SPREAD = (2, 4)


def dot(a, b, contract):
    return lax.dot_general(a, b, ((contract), ((), ())), preferred_element_type=F32)


def turn(x, shift):
    shift = shift % LANES
    return x if shift == 0 else pltpu.roll(x, shift, 1)


def lane_ids(rows):
    return lax.broadcasted_iota(jnp.int32, (rows, LANES), 1)


def pack_tails(tails):
    group = lane_ids(LINE) // TAIL
    packed = tails[0]
    for row in range(1, ROWS):
        packed = jnp.where(group == row, turn(tails[row], TAIL * row), packed)
    return packed


def merge_row(main, tail, row):
    lane = lane_ids(LINE)
    one, two, three = turn(main[1], 32), turn(main[2], 64), turn(main[3], 96)

    def moved(k, to):
        return turn(tail[k], to - TAIL * row)

    return [
        main[0],
        jnp.where(lane < 32, moved(0, 0), one),
        jnp.where(lane < 32, one, jnp.where(lane < 64, moved(1, 32), two)),
        jnp.where(lane < 64, two, jnp.where(lane < 96, moved(2, 64), three)),
        jnp.where(lane < 96, three, moved(3, 96)),
    ]


def split_row(pieces):
    lane = lane_ids(LINE)
    p0, p1, p2, p3, p4 = pieces
    mains = [
        p0,
        jnp.where(lane < 96, turn(p1, -32), turn(p2, -32)),
        jnp.where(lane < 64, turn(p2, -64), turn(p3, -64)),
        jnp.where(lane < 32, turn(p3, 32), turn(p4, 32)),
    ]
    tails = [p1, turn(p2, -32), turn(p3, -64), turn(p4, -96)]
    return mains, tails


def pack_block(dst, main, tails):
    for row in range(ROWS):
        dst[LINE * row : LINE * (row + 1), :] = main(row).astype(dst.dtype)
    dst[PIX:PACK, :] = pack_tails([tails(row) for row in range(ROWS)]).astype(dst.dtype)


def block_kernel(
    nb,
    x_hbm, dy_hbm, gains_hbm, biases_hbm, prior_hbm, counts_hbm, rate_hbm, w1_hbm, w2_hbm,
    out_ref, din_ref, dw_ref, dw2_ref, ng_ref, rs_ref,
    x_ref, dy_ref, gains_ref, biases_ref, prior_ref, counts_ref, rate_ref, w1, w2,
    xf, mid, acc, wide_acc, gact, gpre, prm, prt, a1, g2, gm, gt1, gtz,
    stats0, stats1, stats2, stats3, gx, gat, red0, red1, red_send, own_red,
    d2d_out, d2d_in, part, z_in, z_out,
    ld_sem, st_send, st_recv, pr_send, pr_recv, gx_send, gx_recv, ga_send, ga_recv, za_send, za_recv, gz_send, gz_recv,
    rd_send, rd_recv, ha_send, ha_recv, d2_send, d2_recv, z_send, z_recv, fz_send, fz_recv, fd_send, fd_recv,
    ft_send, ft_recv, product,
    *maps,
):
    b = lax.axis_index("batch")
    h = lax.axis_index("height")
    c = lax.axis_index("chan")
    group = 2 * nb
    me = 2 * b + h
    spread = nb in SPREAD
    home = b if spread else 0
    others = nb - 1 if spread else 0
    along = 1 if spread else 2
    stats, red = (stats0, stats1, stats2, stats3), (red0, red1)
    a2, shares = maps[: others + 1], maps[others + 1 :]

    due, sent = {}, {}

    def drain():
        for f in [*due.values(), *sent.values()]:
            f()

    def arrive(*key):
        due.pop(key)()

    def remote(src, dst, send, recv, to):
        return pltpu.make_async_remote_copy(
            src_ref=src, dst_ref=dst, send_sem=send, recv_sem=recv, device_id=to, device_id_type=MESH
        )

    def over(count, f):
        def run():
            pl.loop(1, count)(f)

        return run

    def at_group(j):
        return (lax.div(j, 2), lax.rem(j, 2), c)

    def at_chan(k):
        return (b, h, k)

    core = (b, 1 - h, c)

    def load(k, src, dst):
        copy = pltpu.make_async_copy(src, dst, ld_sem.at[k])
        copy.start()
        due["load", k] = copy.wait

    for k, (src, dst) in enumerate(
        (
            (x_hbm, x_ref), (counts_hbm, counts_ref), (dy_hbm, dy_ref), (w2_hbm, w2), (gains_hbm, gains_ref),
            (biases_hbm, biases_ref), (w1_hbm, w1), (prior_hbm, prior_ref), (rate_hbm, rate_ref),
        )
    ):
        load(k, src, dst)

    barrier = pltpu.get_barrier_semaphore()

    @pl.loop(1, group)
    def _(d):
        pl.semaphore_signal(barrier, inc=1, device_id=at_group(lax.rem(me + d, group)), device_id_type=MESH)

    @pl.loop(1, CHAN)
    def _(d):
        pl.semaphore_signal(barrier, inc=1, device_id=at_chan(lax.rem(c + d, CHAN)), device_id_type=MESH)

    def line(row):
        return pl.ds(LINE * row, LINE)

    def column_sum(v):
        return jnp.sum(v, axis=0, keepdims=True)

    def stats_copy(e, d):
        j = lax.rem(me + d, group)
        return remote(stats[e].at[j], stats[e].at[j], st_send.at[e, d], st_recv.at[e, j], at_group(j))

    def share_stats(e, first, second):
        stats[e][me, 0:1, :] = first
        stats[e][me, 1:2, :] = second

        @pl.loop(1, group)
        def _(d):
            remote(
                stats[e].at[me], stats[e].at[me], st_send.at[e, d], st_recv.at[e, me],
                at_group(lax.rem(me + d, group)),
            ).start()

        sent["stats", e] = over(group, lambda d: stats_copy(e, d).wait_send())
        due["stats", e] = over(group, lambda d: stats_copy(e, d).wait_recv())

    def sum_stats(e):
        return lax.fori_loop(0, group, lambda j, s: s + stats[e][j], jnp.zeros((8, 2 * LANES), F32))

    def local_stats(src, e):
        here = jnp.full((1, 2 * LANES), count * (ROWS * COLS), jnp.int32).astype(F32)
        s = jnp.zeros((1, 2 * LANES), F32)
        for row in range(ROWS):
            s += column_sum(valid * src[line(row), :])
        mean = s / here
        m2 = jnp.zeros((1, 2 * LANES), F32)
        for row in range(ROWS):
            d = src[line(row), :] - mean
            m2 += column_sum(valid * d * d)
        share_stats(e, s, m2)

    def norm_stats(e):
        tot = sum_stats(e)
        mean = tot[0:1] / total_row

        def scatter(j, s):
            n = jnp.full((1, 2 * LANES), counts_ref[lax.div(j, 2)] * (ROWS * COLS), jnp.int32).astype(F32)
            d = stats[e][j][0:1] / n - mean
            return s + n * d * d

        var = (tot[1:2] + lax.fori_loop(0, group, scatter, jnp.zeros((1, 2 * LANES), F32))) / total_row
        return mean, var

    def sharing(key, block_of, slot, buf, send, recv):
        def copy(d):
            k = lax.rem(c + d, CHAN)
            return remote(block_of(k), slot, send.at[d], recv.at[c], at_chan(k))

        def taken(d):
            k = lax.rem(c + d, CHAN)
            remote(buf(k), buf(k), send.at[d], recv.at[k], at_chan(k)).wait_recv()

        sent[key] = over(CHAN, lambda d: copy(d).wait_send())
        due[key] = over(CHAN, taken)
        return over(CHAN, lambda d: copy(d).start())

    def share(*how):
        sharing(*how)()

    def hand_on(buf, s, send, recv, act):
        for way, to, ok in ((0, b + 1, (s <= b) & (b + 1 < nb)), (1, b - 1, (s >= b) & (b >= 1))):

            @pl.when(ok)
            def _(way=way, to=to):
                act(remote(buf(s), buf(s), send.at[way, s], recv.at[s], (to, h, c)))

    def start(copy):
        copy.start()

    def wait_sent(copy):
        copy.wait_send()

    def from_batch(buf, s, send, recv):
        remote(buf(s), buf(s), send.at[0, s], recv.at[s], (s, h, c)).wait_recv()

    def share_edge(e, buf):
        copy = remote(buf.at[ROWS - (ROWS - 1) * h], buf.at[(ROWS + 1) * h], ha_send.at[e], ha_recv.at[e], core)
        copy.start()
        sent["edge", e] = copy.wait_send
        far = buf.at[(ROWS + 1) * (1 - h)]
        due["edge", e] = remote(far, far, ha_send.at[e], ha_recv.at[e], core).wait_recv

    def clear_borders(buf):
        lanes = buf.shape[2]
        for row in range(1, ROWS + 1):
            buf[row, 0:IMG, :] = jnp.zeros((IMG, lanes), BF16)
            buf[row, IMG + LINE : WIDE, :] = jnp.zeros((IMG, lanes), BF16)
        buf[(ROWS + 1) * h] = jnp.zeros((WIDE, lanes), BF16)

    def window(buf, i, j):
        return buf[pl.ds(i, ROWS), pl.ds(pl.multiple_of(IMG * j, IMG), LINE), :].reshape(PIX, buf.shape[2])

    def conv_taps(i, src, weights):
        @pl.loop(0, 3)
        def _(j):
            acc[:, 0:OWN] += dot(window(src, i, j), weights[3 * i + j], ((1,), (1,)))

    def conv(src, weights, edge):
        acc[...] = jnp.zeros_like(acc)
        conv_taps(1, src, weights)
        if edge is not None:
            arrive("edge", edge)
        conv_taps(0, src, weights)
        conv_taps(2, src, weights)

    def conv_back_taps(i, src, weights):
        @pl.loop(0, 3)
        def _(j):
            wide_acc[...] += dot(window(src, 2 - i, 2 - j), weights[3 * i + j], ((1,), (0,)))

    def conv_back(src, weights, edge, r):
        wide_acc[...] = jnp.zeros_like(wide_acc)
        conv_back_taps(1, src, weights)
        arrive("edge", edge)
        conv_back_taps(0, src, weights)
        conv_back_taps(2, src, weights)
        tails = [[], [], [], []]
        for row in range(ROWS):
            pieces = [wide_acc[line(row), LANES * t : LANES * (t + 1)] for t in range(5)]
            mains, ends = split_row(pieces)
            for k in range(CHAN):
                own_red[k, line(row), :] = mains[k]
                tails[k].append(ends[k])
        for k in range(CHAN):
            own_red[k, PIX:PACK, :] = pack_tails(tails[k])

        @pl.loop(0, CHAN)
        def _(k):
            red_send[r, k] = own_red[k].astype(BF16)

    def share_sums(r):
        share(
            ("red", r), lambda k: red_send.at[r, k], red[r].at[c], lambda k: red[r].at[k], rd_send.at[r], rd_recv.at[r]
        )

    def gather_sum(r):
        arrive("red", r)

        def add(d, s):
            return s + red[r][lax.rem(c + d, CHAN)].astype(F32)

        packed = lax.fori_loop(1, CHAN, add, own_red[c])
        lane = lane_ids(LINE)
        tail = packed[PIX:PACK]
        for row in range(ROWS):
            gact[line(row), 0:LANES] = packed[LINE * row : LINE * (row + 1)]
            gact[line(row), LANES : 2 * LANES] = jnp.where(lane < TAIL, turn(tail, -TAIL * row), 0.0)

    def back_sums(src, mean, inv, gain, bias, e):
        s_gain = jnp.zeros((1, 2 * LANES), F32)
        s_bias = jnp.zeros((1, 2 * LANES), F32)
        for row in range(ROWS):
            hat = (src[line(row), :] - mean) * inv
            pre = gain * hat + bias
            sig = jax.nn.sigmoid(pre)
            grad = gact[line(row), :] * (sig * (1.0 + pre * (1.0 - sig)))
            gpre[line(row), :] = grad
            s_gain += column_sum(valid * grad * hat)
            s_bias += column_sum(valid * grad)
        share_stats(e, s_gain, s_bias)

    def norm_back(src, mean, inv, scale, sums, row):
        hat = (src[line(row), :] - mean) * inv
        return valid * scale * (gpre[line(row), :] - sums[1:2] / total_row - hat * (sums[0:1] / total_row))

    def place(dst, row, pieces):
        for t, piece in enumerate(pieces):
            dst[1 + row, IMG : IMG + LINE, LANES * t : LANES * (t + 1)] = piece.astype(BF16)

    def filter_turn(src, dst):
        for row in range(ROWS):
            flipped = src[1 + row, IMG : IMG + LINE, :].astype(F32).T
            gpre[0:OWN, 0:LANES] = flipped
            dst[0:HALF, line(row)] = gpre[pl.ds(pl.multiple_of(HALF * h, 16), HALF), 0:LANES].astype(BF16)
            dst[HALF:OWN, line(row)] = gpre[pl.ds(pl.multiple_of(HALF * (1 - h), 16), HALF), 0:LANES].astype(BF16)

    def tap_rows(k, t):
        return pl.ds(pl.multiple_of(FLAT * k + HALF * t, 16), HALF)

    def halves(k, t):
        at = TAPS * k + t
        return remote(d2d_out.at[at], d2d_in.at[at], d2_send.at[at], d2_recv.at[at], core)

    def give(k, t, r):
        at = tap_rows(k, t)
        part[at, :] = r[0:HALF]
        d2d_out[TAPS * k + t] = r[HALF:OWN].astype(BF16)
        halves(k, t).start()

    def taps_of(turned, src, first, last, take):
        @pl.loop(first, last)
        def _(t):
            i, j = lax.div(t, 3), lax.rem(t, 3)
            take(t, dot(turned(), window(src, i, j), ((1,), (0,))))

    def halves_sent(k):
        def done():
            @pl.loop(0, TAPS)
            def _(t):
                halves(k, t).wait_send()

        sent["halves", k] = done

    middle = nb // 2
    left = b < middle
    is_end = jnp.logical_or(b == 0, b == nb - 1)
    is_mid = jnp.logical_or(b == middle - 1, b == middle)
    inner = (jnp.where(left, b + 1, b - 1), h, c)
    outer = (jnp.where(left, b - 1, b + 1), h, c)
    steps = along * FLAT // STEP
    mid_off = jnp.where(is_mid, steps, 0)

    def rows_of(q):
        return pl.ds(pl.multiple_of(STEP * q, 16), STEP)

    def inward(q):
        return remote(z_out.at[q], z_in.at[q + mid_off], z_send.at[q], z_recv.at[q + mid_off], inner)

    def total_of(q, half):
        return dw_ref.at[half, q]

    def outward(q):
        return remote(total_of(q, h), total_of(q, h), fz_send.at[q], fz_recv.at[q], outer)

    def across(q):
        return remote(total_of(q, h), total_of(q, h), fd_send.at[q], fd_recv.at[q], core)

    def across_tap(t):
        return remote(dw2_ref.at[h, t], dw2_ref.at[h, t], ft_send.at[t], ft_recv.at[t], core)

    def take_halves(k, g):
        for t in range(3 * g, 3 * g + 3):
            halves(k, t).wait_recv()
            at = tap_rows(k, t)
            part[at, :] = part[at, :] + d2d_in[TAPS * k + t].astype(F32)

        @pl.when(is_end)
        def _():
            first = k * (FLAT // STEP) + 5 * g
            for q in range(first, first + 5):
                z_out[q] = part[rows_of(q), :].astype(BF16)
                inward(q).start()

    def take_final(first, last):
        @pl.loop(first, last)
        def _(t):
            halves(1, t).wait_recv()
            at = tap_rows(1, t)
            dw2_ref[h, t] = (part[at, :] + d2d_in[TAPS + t].astype(F32)).astype(BF16)
            across_tap(t).start()

    def line_step(t):
        @pl.when(jnp.logical_and(t < steps, jnp.logical_not(is_end)))
        def _():
            remote(z_in.at[t], z_in.at[t], z_send.at[t], z_recv.at[t], outer).wait_recv()
            z_out[t] = (part[rows_of(t), :] + z_in[t].astype(F32)).astype(BF16)
            inward(t).start()

        u = t - SKEW

        @pl.when(jnp.logical_and(is_mid, jnp.logical_and(u >= 0, u < steps)))
        def _():
            met = steps + u
            remote(z_in.at[met], z_in.at[met], z_send.at[u], z_recv.at[met], inner).wait_recv()
            dw_ref[h, u] = (z_out[u].astype(F32) + z_in[met].astype(F32)).astype(BF16)

            @pl.when(jnp.logical_not(is_end))
            def _():
                outward(u).start()

            across(u).start()

        v = t - FAR_SKEW

        @pl.when(jnp.logical_and(jnp.logical_not(is_mid), jnp.logical_and(v >= 0, v < steps)))
        def _():
            remote(total_of(v, h), total_of(v, h), fz_send.at[v], fz_recv.at[v], inner).wait_recv()

            @pl.when(jnp.logical_not(is_end))
            def _():
                outward(v).start()

            across(v).start()

    steps_done = [0]

    def line_steps(count):
        first = steps_done[0]
        last = min(first + count, steps + FAR_SKEW)
        if last > first:
            pl.loop(first, last)(line_step)
        steps_done[0] = last

    flip = lax.div(b, max(middle, 1))
    from_end = b + flip * (nb - 1 - 2 * b)

    def source(i):
        s = i + lax.div(i + nb - from_end, nb)
        return s + flip * (nb - 1 - 2 * s)

    sources = [source(i) for i in range(others)]

    def gat_of(s):
        return gat.at[s, c]

    def gtz_of(s):
        return gtz.at[s]

    def share_act(i, s):
        return sharing(
            ("act", i), lambda k: gat.at[s, c], gat.at[s, c], lambda k: gat.at[s, k], ga_send.at[s], ga_recv.at[s]
        )

    def pass_on(first, last):
        for i in range(first, min(last, others)):
            s = sources[i]
            from_batch(gat_of, s, za_send, za_recv)
            hand_on(gat_of, s, za_send, za_recv, start)
            share_act(1 + i, s)()

    def pass_turned(first, last):
        for i in range(first, min(last, others)):
            from_batch(gtz_of, sources[i], gz_send, gz_recv)
            hand_on(gtz_of, sources[i], gz_send, gz_recv, start)

    def inside(f, *a):
        pl.when(jnp.logical_not(is_end))(lambda: f(*a))

    def outside(f, *a):
        pl.when(is_end)(lambda: f(*a))

    def spread_out(i):
        s = home if i == 0 else sources[i - 1]
        arrive("act", i)
        tails = [gat[s, k, PIX:PACK, :].astype(F32) for k in range(CHAN)]
        for row in range(ROWS):
            place(a2[i], row, merge_row([gat[s, k, line(row), :].astype(F32) for k in range(CHAN)], tails, row))
        share_edge(3 + i, a2[i])

    def second_grad(i, first, last):
        s = home if i == 0 else sources[i - 1]
        if first == 0:
            arrive("edge", 3 + i)

        def take(t, r):
            if not spread:
                give(1, t, r)
            elif i % 2 == 0:
                shares[i // 2][t] = r
            else:
                product[...] = r
                both = shares[i // 2][t] + product[...]
                if i < others:
                    shares[i // 2][t] = both
                elif i == 1:
                    give(1, t, both)
                else:
                    give(1, t, shares[0][t] + both)

        taps_of(lambda: gtz[s], a2[i], first, last, take)

    for buf in (g2, a1, gm, *a2):
        clear_borders(buf)
    prm[c] = jnp.zeros((8, 2 * LANES), F32)
    arrive("load", 0)
    xf[:, LANES : 2 * LANES] = jnp.zeros((PIX, LANES), F32)
    xf[:, 0:OWN] = x_ref[...].astype(F32)
    pack_block(gx.at[c], lambda row: xf[line(row), 0:LANES], lambda row: xf[line(row), LANES : 2 * LANES])

    arrive("load", 1)
    count = counts_ref[b]
    valid = (lax.broadcasted_iota(jnp.int32, (LINE, 2 * LANES), 0) % IMG < count).astype(F32)
    total_images = lax.fori_loop(0, nb, lambda i, s: s + counts_ref[i], jnp.int32(0))
    total_row = jnp.full((1, 2 * LANES), total_images * (COLS * COLS), jnp.int32).astype(F32)

    arrive("load", 2)
    for row in range(ROWS):
        g2[1 + row, IMG : IMG + LINE, :] = (dy_ref[line(row), :].astype(F32) * valid[:, 0:OWN]).astype(BF16)

    pl.semaphore_wait(barrier, group - 1 + CHAN - 1)
    share_edge(0, g2)
    local_stats(xf, 0)
    share(("gx",), lambda k: gx.at[c], gx.at[c], lambda k: gx.at[k], gx_send, gx_recv)

    arrive("load", 4)
    arrive("load", 5)
    prm[c, 2:3, 0:OWN] = gains_ref[0:1, :]
    prm[c, 3:4, 0:OWN] = biases_ref[0:1, :]
    prm[c, 4:5, 0:OWN] = gains_ref[1:2, :]
    prm[c, 5:6, 0:OWN] = biases_ref[1:2, :]
    gain1, bias1, gain2, bias2 = (prm[c, k : k + 1, :] for k in range(2, 6))

    filter_turn(g2, gtz.at[home])
    arrive("stats", 0)
    mean1, var1 = norm_stats(0)
    inv1 = lax.rsqrt(var1 + EPSILON)
    prm[c, 0:1, :] = mean1
    prm[c, 1:2, :] = inv1
    share(("prm",), lambda k: prm.at[c], prm.at[c], lambda k: prm.at[k], pr_send, pr_recv)
    if spread:
        hand_on(gtz_of, b, gz_send, gz_recv, start)

    arrive("load", 3)
    conv_back(g2, w2, 0, 0)
    arrive("prm")
    arrive("gx")
    share_sums(0)

    lane8 = lane_ids(8)
    for k in range(CHAN):
        rows = prm[k, :, LANES : 2 * LANES]
        rows = jnp.where(lane8 < TAIL, rows, 0.0)
        prt[k] = rows + turn(rows, TAIL) + turn(rows, 2 * TAIL) + turn(rows, 3 * TAIL)

    def activated(k, at, rows):
        m, i, g, o = (rows[k, r : r + 1, 0:LANES] for r in range(4))
        pre = g * ((gx[k, at, :].astype(F32) - m) * i) + o
        return pre * jax.nn.sigmoid(pre)

    tails = [activated(k, pl.ds(PIX, LINE), prt) for k in range(CHAN)]
    for row in range(ROWS):
        place(a1, row, merge_row([activated(k, line(row), prm) for k in range(CHAN)], tails, row))
    share_edge(1, a1)
    if spread:
        inside(pass_turned, 0, 2)
    arrive("load", 6)
    conv(a1, w1, 1)
    mid[...] = acc[...]

    local_stats(mid, 1)
    gather_sum(0)
    arrive("stats", 1)
    mean2, var2 = norm_stats(1)
    inv2 = lax.rsqrt(var2 + EPSILON)
    back_sums(mid, mean2, inv2, gain2, bias2, 2)

    def activation(row):
        pre = gain2 * ((mid[line(row), :] - mean2) * inv2) + bias2
        return pre * jax.nn.sigmoid(pre)

    acts = [activation(row) for row in range(ROWS)]
    pack_block(gat.at[home, c], lambda row: acts[row][:, 0:LANES], lambda row: acts[row][:, LANES : 2 * LANES])
    share_act(0, home)()
    if spread:
        hand_on(gat_of, b, za_send, za_recv, start)
        inside(pass_turned, 2, others)
    arrive("stats", 2)
    sums2 = sum_stats(2)

    for row in range(ROWS):
        grad = norm_back(mid, mean2, inv2, gain2 * inv2, sums2, row)
        gm[1 + row, IMG : IMG + LINE, :] = grad[:, 0:OWN].astype(BF16)
    share_edge(2, gm)
    filter_turn(gm, gt1)

    def first_grad(g):
        taps_of(lambda: gt1[...], a1, 3 * g, 3 * g + 3, lambda t, r: give(0, t, r))

    first_grad(0)
    first_grad(1)
    take_halves(0, 0)
    first_grad(2)
    take_halves(0, 1)
    halves_sent(0)
    pass_on(0, 1)
    take_halves(0, 2)
    inside(pass_on, 1, 2)
    for i in range(1, others):
        share_act(1 + i, sources[i])

    def work():
        conv_back(gm, w1, 2, 1)
        share_sums(1)
        yield 0
        outside(pass_on, 1, 2)
        inside(pass_on, 2, others)
        spread_out(0)
        if spread:
            outside(pass_turned, 0, others)
        yield 1
        for g in range(3):
            second_grad(0, 3 * g, 3 * g + 3)
            yield 1
        if not spread:
            halves_sent(1)
            for g in range(3):
                take_halves(1, g)
        outside(pass_on, 2, others)
        acc[...] = jnp.zeros_like(acc)
        for i in range(3):
            conv_taps(i, a2[0], w2)
            yield 1
        for row in range(ROWS):
            kept = (xf[line(row), :] + acc[line(row), :]) * valid
            out_ref[line(row), :] = kept[:, 0:OWN].astype(BF16)
        for i in range(1, others + 1):
            spread_out(i)
            yield 1
            if i == min(2, others):
                gather_sum(1)
                back_sums(xf, mean1, inv1, gain1, bias1, 3)
                yield 1
            for g in range(3):
                second_grad(i, 3 * g, 3 * g + 3)
                yield 1
        if not spread:
            gather_sum(1)
            back_sums(xf, mean1, inv1, gain1, bias1, 3)
        if spread:
            halves_sent(1)
            take_final(0, TAPS)
        yield 1

    for count in work():
        line_steps(count)

    arrive("stats", 3)
    sums1 = sum_stats(3)
    for row in range(ROWS):
        grad = norm_back(xf, mean1, inv1, gain1 * inv1, sums1, row)
        din_ref[line(row), :] = (dy_ref[line(row), :].astype(F32) * valid[:, 0:OWN] + grad[:, 0:OWN]).astype(BF16)
    ng_ref[0:2, :] = sums1[0:2, 0:OWN]
    ng_ref[2:4, :] = sums2[0:2, 0:OWN]
    arrive("load", 7)
    arrive("load", 8)
    unbias = total_row / (total_row - 1.0)
    rate = rate_ref[0]
    for k, stat in enumerate((mean1, var1 * unbias, mean2, var2 * unbias)):
        rs_ref[k : k + 1, :] = (1.0 - rate) * prior_ref[k : k + 1, :] + rate * stat[:, 0:OWN]
    line_steps(steps + FAR_SKEW)

    @pl.loop(0, steps)
    def _(q):
        far = total_of(q, 1 - h)
        remote(far, far, fd_send.at[q], fd_recv.at[q], core).wait_recv()

    @pl.loop(0, steps)
    def _(q):
        inward(q).wait_send()
        across(q).wait_send()

        @pl.when(jnp.logical_not(is_end))
        def _():
            outward(q).wait_send()

    if spread:

        @pl.loop(0, TAPS)
        def _(t):
            far = dw2_ref.at[1 - h, t]
            remote(far, far, ft_send.at[t], ft_recv.at[t], core).wait_recv()
            across_tap(t).wait_send()

        for s in (b, *sources):
            hand_on(gat_of, s, za_send, za_recv, wait_sent)
            hand_on(gtz_of, s, gz_send, gz_recv, wait_sent)
    drain()


def finish_kernel(
    dw1, dw2, out, din, ng, rs, out_to, din_to, dw1_to, dw2_to, ng_to, rs_to, wide, big_sem, small_sem
):
    small = [
        pltpu.make_async_copy(src, dst, small_sem.at[k])
        for k, (src, dst) in enumerate(((out, out_to), (din, din_to), (ng, ng_to), (rs, rs_to)))
    ]
    for copy in small:
        copy.start()

    def write(k, t, half):
        to = (dw1_to, dw2_to)[k]
        return pltpu.make_async_copy(wide.at[k, t, half], to.at[t, pl.ds(HALF * half, HALF)], big_sem.at[k, t, half])

    for k in range(2):

        @pl.loop(0, TAPS)
        def _(t, k=k):
            for half in range(2):
                wide[k, t, half] = (dw1, dw2)[k][half, pl.ds(pl.multiple_of(HALF * t, 16), HALF), :].astype(F32)
                write(k, t, half).start()

    for k in range(2):

        @pl.loop(0, TAPS)
        def _(t, k=k):
            for half in range(2):
                write(k, t, half).wait()

    for copy in small:
        copy.wait()


def shards(features, gains, biases, conv_one, conv_two, out_grad, counts, running_prior, momentum):
    nb = lax.axis_size("batch")
    group = 2 * nb
    spread = nb in SPREAD
    along = 1 if spread else 2
    steps = along * FLAT // STEP
    sources = nb if spread else 1
    hbm = pl.BlockSpec(memory_space=pltpu.HBM)
    in_vmem = pl.BlockSpec(memory_space=pltpu.VMEM)
    dma = pltpu.SemaphoreType.DMA
    vmem = pltpu.VMEM
    maps_out = jax.ShapeDtypeStruct((PIX, OWN), BF16)
    rows_out = jax.ShapeDtypeStruct((4, OWN), F32)
    out, din, dw, dw2, ng, rs = pl.pallas_call(
        functools.partial(block_kernel, nb),
        out_shape=(
            vmem((PIX, OWN), BF16),
            vmem((PIX, OWN), BF16),
            vmem((2, steps, STEP, FULL), BF16),
            vmem((2, TAPS, HALF, FULL) if spread else (8, LANES), BF16 if spread else F32),
            vmem((4, OWN), F32),
            vmem((4, OWN), F32),
        ),
        in_specs=[hbm] * 9,
        out_specs=(in_vmem,) * 6,
        scratch_shapes=[
            vmem((PIX, OWN), BF16),
            vmem((PIX, OWN), BF16),
            vmem((2, OWN), F32),
            vmem((2, OWN), F32),
            vmem((4, OWN), F32),
            pltpu.SMEM((nb,), jnp.int32),
            pltpu.SMEM((1,), F32),
            vmem((TAPS, OWN, FULL), BF16),
            vmem((TAPS, OWN, FULL), BF16),
            vmem((PIX, 2 * LANES), F32),
            vmem((PIX, 2 * LANES), F32),
            vmem((PIX, 2 * LANES), F32),
            vmem((PIX, FULL), F32),
            vmem((PIX, 2 * LANES), F32),
            vmem((PIX, 2 * LANES), F32),
            vmem((CHAN, 8, 2 * LANES), F32),
            vmem((CHAN, 8, LANES), F32),
            vmem((ROWS + 2, WIDE, FULL), BF16),
            vmem((ROWS + 2, WIDE, OWN), BF16),
            vmem((ROWS + 2, WIDE, OWN), BF16),
            vmem((OWN, PIX), BF16),
            vmem((sources, OWN, PIX), BF16),
            *[vmem((group, 8, 2 * LANES), F32)] * 4,
            vmem((CHAN, PACK, LANES), BF16),
            vmem((sources, CHAN, PACK, LANES), BF16),
            *[vmem((CHAN, PACK, LANES), BF16)] * 2,
            vmem((2, CHAN, PACK, LANES), BF16),
            vmem((CHAN, PACK, LANES), F32),
            *[vmem((CHUNKS, HALF, FULL), BF16)] * 2,
            vmem((2 * FLAT, FULL), F32),
            vmem((2 * steps, STEP, FULL), BF16),
            vmem((steps, STEP, FULL), BF16),
            dma((9,)),
            dma((4, group)),
            dma((4, group)),
            *[dma((CHAN,))] * 4,
            *[dma((sources, CHAN))] * 2,
            *[dma((2, nb)), dma((nb,))] * 2,
            *[dma((2, CHAN))] * 2,
            *[dma((3 + sources,))] * 2,
            *[dma((CHUNKS,))] * 2,
            dma((steps,)),
            dma((2 * steps,)),
            *[dma((steps,))] * 4,
            *[dma((TAPS,))] * 2,
            vmem((OWN, FULL), F32),
            *[vmem((ROWS + 2, WIDE, FULL), BF16)] * sources,
            *[vmem((TAPS, OWN, FULL), F32)] * (sources // 2),
        ],
        compiler_params=pltpu.CompilerParams(
            collective_id=0, has_side_effects=True, vmem_limit_bytes=55 * 1024 * 1024
        ),
    )(
        features.reshape(PIX, OWN),
        out_grad.reshape(PIX, OWN),
        gains,
        biases,
        running_prior,
        counts,
        momentum,
        jnp.transpose(conv_one, (1, 2, 0, 3)).reshape(TAPS, OWN, FULL),
        jnp.transpose(conv_two, (1, 2, 0, 3)).reshape(TAPS, OWN, FULL),
    )
    if spread:
        dw1 = dw.reshape(2, FLAT, FULL)
        dw2 = dw2.reshape(2, FLAT, FULL)
    else:
        both = dw.reshape(2, 2, FLAT, FULL)
        dw1, dw2 = both[:, 0], both[:, 1]
    filters_out = jax.ShapeDtypeStruct((TAPS, OWN, FULL), F32)
    out, din, first, second, ng, rs = pl.pallas_call(
        finish_kernel,
        out_shape=(maps_out, maps_out, filters_out, filters_out, rows_out, rows_out),
        in_specs=[in_vmem] * 6,
        out_specs=(hbm,) * 6,
        scratch_shapes=[vmem((2, TAPS, 2, HALF, FULL), F32), dma((2, TAPS, 2)), dma((4,))],
        compiler_params=pltpu.CompilerParams(vmem_limit_bytes=32 * 1024 * 1024),
    )(dw1, dw2, out, din, ng, rs)
    maps = (ROWS, COLS, IMG, OWN)

    def filters(taps):
        return jnp.transpose(taps.reshape(3, 3, OWN, FULL), (2, 0, 1, 3))

    return (out.reshape(maps), din.reshape(maps), filters(first), filters(second), ng, rs)


def solution(mesh):
    maps = P("height", None, "batch", "chan")
    rows = P(None, "chan")
    filters = P("chan", None, None, None)
    return jax.shard_map(
        shards,
        mesh=mesh,
        in_specs=(maps, rows, rows, filters, filters, maps, P(), rows, P()),
        out_specs=(maps, maps, filters, filters, rows, rows),
        check_vma=False,
    )
```

```python
import functools

import jax
import jax.numpy as jnp
from jax import lax
from jax.experimental import pallas as pl
from jax.experimental.pallas import tpu as pltpu
from jax.sharding import PartitionSpec as P

MESH = pl.DeviceIdType.MESH
EPSILON = 1e-05
F32 = jnp.float32
BF16 = jnp.bfloat16

CHAN = 4
ROWS = 4
COLS = 8
IMG = 16
LINE = COLS * IMG
PIX = ROWS * LINE
WIDE = LINE + 2 * IMG
OWN = 160
FULL = CHAN * OWN
LANES = 128
TAIL = OWN - LANES
PACK = PIX + LINE
HALF = OWN // 2
TAPS = 9
CHUNKS = 2 * TAPS
FLAT = TAPS * HALF
STEP = 48
THREE = 3 * HALF
SKEW = 3
FAR_SKEW = 6
SPREAD = (2, 4)


def dot(a, b, contract):
    return lax.dot_general(a, b, ((contract), ((), ())), preferred_element_type=F32)


def turn(x, shift):
    shift = shift % LANES
    return x if shift == 0 else pltpu.roll(x, shift, 1)


def lane_ids(rows):
    return lax.broadcasted_iota(jnp.int32, (rows, LANES), 1)


def pack_tails(tails):
    group = lane_ids(LINE) // TAIL
    packed = tails[0]
    for row in range(1, ROWS):
        packed = jnp.where(group == row, turn(tails[row], TAIL * row), packed)
    return packed


def merge_row(main, tail, row):
    lane = lane_ids(LINE)
    one, two, three = turn(main[1], 32), turn(main[2], 64), turn(main[3], 96)

    def moved(k, to):
        return turn(tail[k], to - TAIL * row)

    return [
        main[0],
        jnp.where(lane < 32, moved(0, 0), one),
        jnp.where(lane < 32, one, jnp.where(lane < 64, moved(1, 32), two)),
        jnp.where(lane < 64, two, jnp.where(lane < 96, moved(2, 64), three)),
        jnp.where(lane < 96, three, moved(3, 96)),
    ]


def split_row(pieces):
    lane = lane_ids(LINE)
    p0, p1, p2, p3, p4 = pieces
    mains = [
        p0,
        jnp.where(lane < 96, turn(p1, -32), turn(p2, -32)),
        jnp.where(lane < 64, turn(p2, -64), turn(p3, -64)),
        jnp.where(lane < 32, turn(p3, 32), turn(p4, 32)),
    ]
    tails = [p1, turn(p2, -32), turn(p3, -64), turn(p4, -96)]
    return mains, tails


def pack_block(dst, main, tails):
    for row in range(ROWS):
        dst[LINE * row : LINE * (row + 1), :] = main(row).astype(dst.dtype)
    dst[PIX:PACK, :] = pack_tails([tails(row) for row in range(ROWS)]).astype(dst.dtype)


def block_kernel(
    nb,
    x_hbm, dy_hbm, gains_hbm, biases_hbm, prior_hbm, counts_hbm, rate_hbm, w1_hbm, w2_hbm,
    out_ref, din_ref, dw_ref, dw2_ref, ng_ref, rs_ref,
    x_ref, dy_ref, gains_ref, biases_ref, prior_ref, counts_ref, rate_ref, w1, w2,
    xf, mid, acc, wide_acc, gact, gpre, prm, prt, a1, g2, gm, gt1, gtz,
    stats0, stats1, stats2, stats3, gx, gat, red0, red1, red_send, own_red,
    d2d_out, d2d_in, part, z_in, z_out,
    ld_sem, st_send, st_recv, pr_send, pr_recv, gx_send, gx_recv, ga_send, ga_recv, za_send, za_recv, gz_send, gz_recv,
    rd_send, rd_recv, ha_send, ha_recv, d2_send, d2_recv, z_send, z_recv, fz_send, fz_recv, fd_send, fd_recv,
    ft_send, ft_recv, product,
    *maps,
):
    b = lax.axis_index("batch")
    h = lax.axis_index("height")
    c = lax.axis_index("chan")
    group = 2 * nb
    me = 2 * b + h
    spread = nb in SPREAD
    home = b if spread else 0
    others = nb - 1 if spread else 0
    along = 1 if spread else 2
    stats, red = (stats0, stats1, stats2, stats3), (red0, red1)
    a2, shares = maps[: others + 1], maps[others + 1 :]

    due, sent = {}, {}

    def drain():
        for f in [*due.values(), *sent.values()]:
            f()

    def arrive(*key):
        due.pop(key)()

    def remote(src, dst, send, recv, to):
        return pltpu.make_async_remote_copy(
            src_ref=src, dst_ref=dst, send_sem=send, recv_sem=recv, device_id=to, device_id_type=MESH
        )

    def over(count, f):
        def run():
            pl.loop(1, count)(f)

        return run

    def at_group(j):
        return (lax.div(j, 2), lax.rem(j, 2), c)

    def at_chan(k):
        return (b, h, k)

    core = (b, 1 - h, c)

    def load(k, src, dst):
        copy = pltpu.make_async_copy(src, dst, ld_sem.at[k])
        copy.start()
        due["load", k] = copy.wait

    for k, (src, dst) in enumerate(
        (
            (x_hbm, x_ref), (counts_hbm, counts_ref), (dy_hbm, dy_ref), (w2_hbm, w2), (gains_hbm, gains_ref),
            (biases_hbm, biases_ref), (w1_hbm, w1), (prior_hbm, prior_ref), (rate_hbm, rate_ref),
        )
    ):
        load(k, src, dst)

    barrier = pltpu.get_barrier_semaphore()

    @pl.loop(1, group)
    def _(d):
        pl.semaphore_signal(barrier, inc=1, device_id=at_group(lax.rem(me + d, group)), device_id_type=MESH)

    @pl.loop(1, CHAN)
    def _(d):
        pl.semaphore_signal(barrier, inc=1, device_id=at_chan(lax.rem(c + d, CHAN)), device_id_type=MESH)

    def line(row):
        return pl.ds(LINE * row, LINE)

    def column_sum(v):
        return jnp.sum(v, axis=0, keepdims=True)

    def stats_copy(e, d):
        j = lax.rem(me + d, group)
        return remote(stats[e].at[j], stats[e].at[j], st_send.at[e, d], st_recv.at[e, j], at_group(j))

    def share_stats(e, first, second):
        stats[e][me, 0:1, :] = first
        stats[e][me, 1:2, :] = second

        @pl.loop(1, group)
        def _(d):
            remote(
                stats[e].at[me], stats[e].at[me], st_send.at[e, d], st_recv.at[e, me],
                at_group(lax.rem(me + d, group)),
            ).start()

        sent["stats", e] = over(group, lambda d: stats_copy(e, d).wait_send())
        due["stats", e] = over(group, lambda d: stats_copy(e, d).wait_recv())

    def sum_stats(e):
        return lax.fori_loop(0, group, lambda j, s: s + stats[e][j], jnp.zeros((8, 2 * LANES), F32))

    def local_stats(src, e):
        here = jnp.full((1, 2 * LANES), count * (ROWS * COLS), jnp.int32).astype(F32)
        s = jnp.zeros((1, 2 * LANES), F32)
        for row in range(ROWS):
            s += column_sum(valid * src[line(row), :])
        mean = s / here
        m2 = jnp.zeros((1, 2 * LANES), F32)
        for row in range(ROWS):
            d = src[line(row), :] - mean
            m2 += column_sum(valid * d * d)
        share_stats(e, s, m2)

    def norm_stats(e):
        tot = sum_stats(e)
        mean = tot[0:1] / total_row

        def scatter(j, s):
            n = jnp.full((1, 2 * LANES), counts_ref[lax.div(j, 2)] * (ROWS * COLS), jnp.int32).astype(F32)
            d = stats[e][j][0:1] / n - mean
            return s + n * d * d

        var = (tot[1:2] + lax.fori_loop(0, group, scatter, jnp.zeros((1, 2 * LANES), F32))) / total_row
        return mean, var

    def sharing(key, block_of, slot, buf, send, recv):
        def copy(d):
            k = lax.rem(c + d, CHAN)
            return remote(block_of(k), slot, send.at[d], recv.at[c], at_chan(k))

        def taken(d):
            k = lax.rem(c + d, CHAN)
            remote(buf(k), buf(k), send.at[d], recv.at[k], at_chan(k)).wait_recv()

        sent[key] = over(CHAN, lambda d: copy(d).wait_send())
        due[key] = over(CHAN, taken)
        return over(CHAN, lambda d: copy(d).start())

    def share(*how):
        sharing(*how)()

    def hand_on(buf, s, send, recv, act):
        for way, to, ok in ((0, b + 1, (s <= b) & (b + 1 < nb)), (1, b - 1, (s >= b) & (b >= 1))):

            @pl.when(ok)
            def _(way=way, to=to):
                act(remote(buf(s), buf(s), send.at[way, s], recv.at[s], (to, h, c)))

    def start(copy):
        copy.start()

    def wait_sent(copy):
        copy.wait_send()

    def from_batch(buf, s, send, recv):
        remote(buf(s), buf(s), send.at[0, s], recv.at[s], (s, h, c)).wait_recv()

    def share_edge(e, buf):
        copy = remote(buf.at[ROWS - (ROWS - 1) * h], buf.at[(ROWS + 1) * h], ha_send.at[e], ha_recv.at[e], core)
        copy.start()
        sent["edge", e] = copy.wait_send
        far = buf.at[(ROWS + 1) * (1 - h)]
        due["edge", e] = remote(far, far, ha_send.at[e], ha_recv.at[e], core).wait_recv

    def clear_borders(buf):
        lanes = buf.shape[2]
        for row in range(1, ROWS + 1):
            buf[row, 0:IMG, :] = jnp.zeros((IMG, lanes), BF16)
            buf[row, IMG + LINE : WIDE, :] = jnp.zeros((IMG, lanes), BF16)
        buf[(ROWS + 1) * h] = jnp.zeros((WIDE, lanes), BF16)

    def window(buf, i, j):
        return buf[pl.ds(i, ROWS), pl.ds(pl.multiple_of(IMG * j, IMG), LINE), :].reshape(PIX, buf.shape[2])

    def conv_taps(i, src, weights):
        @pl.loop(0, 3)
        def _(j):
            acc[:, 0:OWN] += dot(window(src, i, j), weights[3 * i + j], ((1,), (1,)))

    def conv(src, weights, edge):
        acc[...] = jnp.zeros_like(acc)
        conv_taps(1, src, weights)
        if edge is not None:
            arrive("edge", edge)
        conv_taps(0, src, weights)
        conv_taps(2, src, weights)

    def conv_back_taps(i, src, weights):
        @pl.loop(0, 3)
        def _(j):
            wide_acc[...] += dot(window(src, 2 - i, 2 - j), weights[3 * i + j], ((1,), (0,)))

    def conv_back(src, weights, edge, r):
        wide_acc[...] = jnp.zeros_like(wide_acc)
        conv_back_taps(1, src, weights)
        arrive("edge", edge)
        conv_back_taps(0, src, weights)
        conv_back_taps(2, src, weights)
        back_split(r)

    def back_split(r):
        tails = [[], [], [], []]
        for row in range(ROWS):
            pieces = [wide_acc[line(row), LANES * t : LANES * (t + 1)] for t in range(5)]
            mains, ends = split_row(pieces)
            for k in range(CHAN):
                own_red[k, line(row), :] = mains[k]
                tails[k].append(ends[k])
        for k in range(CHAN):
            own_red[k, PIX:PACK, :] = pack_tails(tails[k])

        @pl.loop(0, CHAN)
        def _(k):
            red_send[r, k] = own_red[k].astype(BF16)

    def share_sums(r):
        share(
            ("red", r), lambda k: red_send.at[r, k], red[r].at[c], lambda k: red[r].at[k], rd_send.at[r], rd_recv.at[r]
        )

    def gather_sum(r):
        arrive("red", r)

        def add(d, s):
            return s + red[r][lax.rem(c + d, CHAN)].astype(F32)

        packed = lax.fori_loop(1, CHAN, add, own_red[c])
        lane = lane_ids(LINE)
        tail = packed[PIX:PACK]
        for row in range(ROWS):
            gact[line(row), 0:LANES] = packed[LINE * row : LINE * (row + 1)]
            gact[line(row), LANES : 2 * LANES] = jnp.where(lane < TAIL, turn(tail, -TAIL * row), 0.0)

    def back_sums(src, mean, inv, gain, bias, e):
        s_gain = jnp.zeros((1, 2 * LANES), F32)
        s_bias = jnp.zeros((1, 2 * LANES), F32)
        for row in range(ROWS):
            hat = (src[line(row), :] - mean) * inv
            pre = gain * hat + bias
            sig = jax.nn.sigmoid(pre)
            grad = gact[line(row), :] * (sig * (1.0 + pre * (1.0 - sig)))
            gpre[line(row), :] = grad
            s_gain += column_sum(valid * grad * hat)
            s_bias += column_sum(valid * grad)
        share_stats(e, s_gain, s_bias)

    def norm_back(src, mean, inv, scale, sums, row):
        hat = (src[line(row), :] - mean) * inv
        return valid * scale * (gpre[line(row), :] - sums[1:2] / total_row - hat * (sums[0:1] / total_row))

    def place(dst, row, pieces):
        for t, piece in enumerate(pieces):
            dst[1 + row, IMG : IMG + LINE, LANES * t : LANES * (t + 1)] = piece.astype(BF16)

    def filter_turn(src, dst):
        for row in range(ROWS):
            flipped = src[1 + row, IMG : IMG + LINE, :].astype(F32).T
            gpre[0:OWN, 0:LANES] = flipped
            dst[0:HALF, line(row)] = gpre[pl.ds(pl.multiple_of(HALF * h, 16), HALF), 0:LANES].astype(BF16)
            dst[HALF:OWN, line(row)] = gpre[pl.ds(pl.multiple_of(HALF * (1 - h), 16), HALF), 0:LANES].astype(BF16)

    def tap_rows(k, t):
        return pl.ds(pl.multiple_of(FLAT * k + HALF * t, 16), HALF)

    def halves(k, t):
        at = TAPS * k + t
        return remote(d2d_out.at[at], d2d_in.at[at], d2_send.at[at], d2_recv.at[at], core)

    def give(k, t, r):
        at = tap_rows(k, t)
        part[at, :] = r[0:HALF]
        d2d_out[TAPS * k + t] = r[HALF:OWN].astype(BF16)
        halves(k, t).start()

    def taps_of(turned, src, first, last, take):
        for i in range(first // 3, last // 3):

            @pl.loop(0, 3)
            def _(j, i=i):
                take(3 * i + j, dot(turned(), window(src, i, j), ((1,), (0,))))

    def halves_sent(k):
        def done():
            @pl.loop(0, TAPS)
            def _(t):
                halves(k, t).wait_send()

        sent["halves", k] = done

    middle = nb // 2
    left = b < middle
    is_end = jnp.logical_or(b == 0, b == nb - 1)
    is_mid = jnp.logical_or(b == middle - 1, b == middle)
    inner = (jnp.where(left, b + 1, b - 1), h, c)
    outer = (jnp.where(left, b - 1, b + 1), h, c)
    steps = along * FLAT // STEP
    mid_off = jnp.where(is_mid, steps, 0)

    def rows_of(q):
        return pl.ds(pl.multiple_of(STEP * q, 16), STEP)

    def inward(q):
        return remote(z_out.at[q], z_in.at[q + mid_off], z_send.at[q], z_recv.at[q + mid_off], inner)

    def total_of(q, half):
        return dw_ref.at[half, q]

    def outward(q):
        return remote(total_of(q, h), total_of(q, h), fz_send.at[q], fz_recv.at[q], outer)

    def across(q):
        return remote(total_of(q, h), total_of(q, h), fd_send.at[q], fd_recv.at[q], core)

    def across_tap(t):
        return remote(dw2_ref.at[h, t], dw2_ref.at[h, t], ft_send.at[t], ft_recv.at[t], core)

    def take_halves(k, g):
        for t in range(3 * g, 3 * g + 3):
            halves(k, t).wait_recv()
            at = tap_rows(k, t)
            part[at, :] = part[at, :] + d2d_in[TAPS * k + t].astype(F32)

        @pl.when(is_end)
        def _():
            first = k * (FLAT // STEP) + 5 * g
            for q in range(first, first + 5):
                z_out[q] = part[rows_of(q), :].astype(BF16)
                inward(q).start()

    def take_final(first, last):
        @pl.loop(first, last)
        def _(t):
            halves(1, t).wait_recv()
            at = tap_rows(1, t)
            dw2_ref[h, t] = (part[at, :] + d2d_in[TAPS + t].astype(F32)).astype(BF16)
            across_tap(t).start()

    def line_step(t):
        @pl.when(jnp.logical_and(t < steps, jnp.logical_not(is_end)))
        def _():
            remote(z_in.at[t], z_in.at[t], z_send.at[t], z_recv.at[t], outer).wait_recv()
            z_out[t] = (part[rows_of(t), :] + z_in[t].astype(F32)).astype(BF16)
            inward(t).start()

        u = t - SKEW

        @pl.when(jnp.logical_and(is_mid, jnp.logical_and(u >= 0, u < steps)))
        def _():
            met = steps + u
            remote(z_in.at[met], z_in.at[met], z_send.at[u], z_recv.at[met], inner).wait_recv()
            dw_ref[h, u] = (z_out[u].astype(F32) + z_in[met].astype(F32)).astype(BF16)

            @pl.when(jnp.logical_not(is_end))
            def _():
                outward(u).start()

            across(u).start()

        v = t - FAR_SKEW

        @pl.when(jnp.logical_and(jnp.logical_not(is_mid), jnp.logical_and(v >= 0, v < steps)))
        def _():
            remote(total_of(v, h), total_of(v, h), fz_send.at[v], fz_recv.at[v], inner).wait_recv()

            @pl.when(jnp.logical_not(is_end))
            def _():
                outward(v).start()

            across(v).start()

    steps_done = [0]

    def line_steps(count):
        first = steps_done[0]
        last = min(first + count, steps + FAR_SKEW)
        if last > first:
            pl.loop(first, last)(line_step)
        steps_done[0] = last

    flip = lax.div(b, max(middle, 1))
    from_end = b + flip * (nb - 1 - 2 * b)

    def source(i):
        s = i + lax.div(i + nb - from_end, nb)
        return s + flip * (nb - 1 - 2 * s)

    sources = [source(i) for i in range(others)]

    def gat_of(s):
        return gat.at[s, c]

    def gtz_of(s):
        return gtz.at[s]

    def share_act(i, s):
        return sharing(
            ("act", i), lambda k: gat.at[s, c], gat.at[s, c], lambda k: gat.at[s, k], ga_send.at[s], ga_recv.at[s]
        )

    def pass_on(first, last):
        for i in range(first, min(last, others)):
            s = sources[i]
            from_batch(gat_of, s, za_send, za_recv)
            hand_on(gat_of, s, za_send, za_recv, start)
            share_act(1 + i, s)()

    def pass_turned(first, last):
        for i in range(first, min(last, others)):
            from_batch(gtz_of, sources[i], gz_send, gz_recv)
            hand_on(gtz_of, sources[i], gz_send, gz_recv, start)

    def inside(f, *a):
        pl.when(jnp.logical_not(is_end))(lambda: f(*a))

    def outside(f, *a):
        pl.when(is_end)(lambda: f(*a))

    def spread_out(i):
        s = home if i == 0 else sources[i - 1]
        arrive("act", i)
        tails = [gat[s, k, PIX:PACK, :].astype(F32) for k in range(CHAN)]
        for row in range(ROWS):
            place(a2[i], row, merge_row([gat[s, k, line(row), :].astype(F32) for k in range(CHAN)], tails, row))
        share_edge(3 + i, a2[i])

    def second_grad(i, first, last):
        s = home if i == 0 else sources[i - 1]
        def take(t, r):
            if not spread:
                give(1, t, r)
            elif i % 2 == 0:
                shares[i // 2][t] = r
            else:
                product[...] = r
                both = shares[i // 2][t] + product[...]
                if i < others:
                    shares[i // 2][t] = both
                elif i == 1:
                    give(1, t, both)
                else:
                    give(1, t, shares[0][t] + both)

        taps_of(lambda: gtz[s], a2[i], first, last, take)

    for buf in (g2, a1, gm, *a2):
        clear_borders(buf)
    prm[c] = jnp.zeros((8, 2 * LANES), F32)
    arrive("load", 0)
    xf[:, LANES : 2 * LANES] = jnp.zeros((PIX, LANES), F32)
    xf[:, 0:OWN] = x_ref[...].astype(F32)
    pack_block(gx.at[c], lambda row: xf[line(row), 0:LANES], lambda row: xf[line(row), LANES : 2 * LANES])

    arrive("load", 1)
    count = counts_ref[b]
    valid = (lax.broadcasted_iota(jnp.int32, (LINE, 2 * LANES), 0) % IMG < count).astype(F32)
    total_images = lax.fori_loop(0, nb, lambda i, s: s + counts_ref[i], jnp.int32(0))
    total_row = jnp.full((1, 2 * LANES), total_images * (COLS * COLS), jnp.int32).astype(F32)

    arrive("load", 2)
    for row in range(ROWS):
        g2[1 + row, IMG : IMG + LINE, :] = (dy_ref[line(row), :].astype(F32) * valid[:, 0:OWN]).astype(BF16)

    pl.semaphore_wait(barrier, group - 1 + CHAN - 1)
    share_edge(0, g2)
    local_stats(xf, 0)
    share(("gx",), lambda k: gx.at[c], gx.at[c], lambda k: gx.at[k], gx_send, gx_recv)

    arrive("load", 4)
    arrive("load", 5)
    prm[c, 2:3, 0:OWN] = gains_ref[0:1, :]
    prm[c, 3:4, 0:OWN] = biases_ref[0:1, :]
    prm[c, 4:5, 0:OWN] = gains_ref[1:2, :]
    prm[c, 5:6, 0:OWN] = biases_ref[1:2, :]
    gain1, bias1, gain2, bias2 = (prm[c, k : k + 1, :] for k in range(2, 6))

    filter_turn(g2, gtz.at[home])
    arrive("stats", 0)
    mean1, var1 = norm_stats(0)
    inv1 = lax.rsqrt(var1 + EPSILON)
    prm[c, 0:1, :] = mean1
    prm[c, 1:2, :] = inv1
    share(("prm",), lambda k: prm.at[c], prm.at[c], lambda k: prm.at[k], pr_send, pr_recv)
    if spread:
        hand_on(gtz_of, b, gz_send, gz_recv, start)

    arrive("load", 3)
    conv_back(g2, w2, 0, 0)
    share_sums(0)
    arrive("prm")
    arrive("gx")

    lane8 = lane_ids(8)
    for k in range(CHAN):
        rows = prm[k, :, LANES : 2 * LANES]
        rows = jnp.where(lane8 < TAIL, rows, 0.0)
        prt[k] = rows + turn(rows, TAIL) + turn(rows, 2 * TAIL) + turn(rows, 3 * TAIL)

    def activated(k, at, rows):
        m, i, g, o = (rows[k, r : r + 1, 0:LANES] for r in range(4))
        pre = g * ((gx[k, at, :].astype(F32) - m) * i) + o
        return pre * jax.nn.sigmoid(pre)

    tails = [activated(k, pl.ds(PIX, LINE), prt) for k in range(CHAN)]
    for row in range(ROWS):
        place(a1, row, merge_row([activated(k, line(row), prm) for k in range(CHAN)], tails, row))
    share_edge(1, a1)
    if spread:
        inside(pass_turned, 0, 2)
    arrive("load", 6)
    conv(a1, w1, 1)
    mid[...] = acc[...]

    local_stats(mid, 1)
    arrive("stats", 1)
    mean2, var2 = norm_stats(1)
    inv2 = lax.rsqrt(var2 + EPSILON)
    def activation(row):
        pre = gain2 * ((mid[line(row), :] - mean2) * inv2) + bias2
        return pre * jax.nn.sigmoid(pre)

    acts = [activation(row) for row in range(ROWS)]
    pack_block(gat.at[home, c], lambda row: acts[row][:, 0:LANES], lambda row: acts[row][:, LANES : 2 * LANES])
    share_act(0, home)()
    gather_sum(0)
    back_sums(mid, mean2, inv2, gain2, bias2, 2)
    if spread:
        hand_on(gat_of, b, za_send, za_recv, start)
        inside(pass_turned, 2, others)
    arrive("stats", 2)
    sums2 = sum_stats(2)

    for row in range(ROWS):
        grad = norm_back(mid, mean2, inv2, gain2 * inv2, sums2, row)
        gm[1 + row, IMG : IMG + LINE, :] = grad[:, 0:OWN].astype(BF16)
    share_edge(2, gm)
    filter_turn(gm, gt1)

    def first_grad(g):
        taps_of(lambda: gt1[...], a1, 3 * g, 3 * g + 3, lambda t, r: give(0, t, r))

    first_grad(0)
    first_grad(1)
    take_halves(0, 0)
    first_grad(2)
    take_halves(0, 1)
    halves_sent(0)
    pass_on(0, 1)
    take_halves(0, 2)
    inside(pass_on, 1, 2)
    for i in range(1, others):
        share_act(1 + i, sources[i])

    def work():
        wide_acc[...] = jnp.zeros_like(wide_acc)
        conv_back_taps(1, gm, w1)
        arrive("edge", 2)
        conv_back_taps(0, gm, w1)
        yield 1
        conv_back_taps(2, gm, w1)
        back_split(1)
        share_sums(1)
        yield 1
        outside(pass_on, 1, 2)
        inside(pass_on, 2, others)
        spread_out(0)
        if spread:
            outside(pass_turned, 0, others)
        yield 1
        for n, g in enumerate((1, 0, 2)):
            if n == 1:
                arrive("edge", 3)
            second_grad(0, 3 * g, 3 * g + 3)
            yield 1
        if not spread:
            halves_sent(1)
            for g in range(3):
                take_halves(1, g)
        outside(pass_on, 2, others)
        acc[...] = jnp.zeros_like(acc)
        for i in range(3):
            conv_taps(i, a2[0], w2)
            yield 1
        for row in range(ROWS):
            kept = (xf[line(row), :] + acc[line(row), :]) * valid
            out_ref[line(row), :] = kept[:, 0:OWN].astype(BF16)
        for i in range(1, others + 1):
            spread_out(i)
            yield 1
            if i == min(2, others):
                gather_sum(1)
                back_sums(xf, mean1, inv1, gain1, bias1, 3)
                yield 1
            for n, g in enumerate((1, 0, 2)):
                if n == 1:
                    arrive("edge", 3 + i)
                second_grad(i, 3 * g, 3 * g + 3)
                if i == others and n > 0:
                    last = (1, 0)[n - 1]
                    take_final(3 * last, 3 * last + 3)
                yield 1
        if not spread:
            gather_sum(1)
            back_sums(xf, mean1, inv1, gain1, bias1, 3)
        if spread:
            halves_sent(1)
            take_final(6, TAPS)
        yield 1

    for count in work():
        line_steps(count)

    arrive("stats", 3)
    sums1 = sum_stats(3)
    for row in range(ROWS):
        grad = norm_back(xf, mean1, inv1, gain1 * inv1, sums1, row)
        din_ref[line(row), :] = (dy_ref[line(row), :].astype(F32) * valid[:, 0:OWN] + grad[:, 0:OWN]).astype(BF16)
    ng_ref[0:2, :] = sums1[0:2, 0:OWN]
    ng_ref[2:4, :] = sums2[0:2, 0:OWN]
    arrive("load", 7)
    arrive("load", 8)
    unbias = total_row / (total_row - 1.0)
    rate = rate_ref[0]
    for k, stat in enumerate((mean1, var1 * unbias, mean2, var2 * unbias)):
        rs_ref[k : k + 1, :] = (1.0 - rate) * prior_ref[k : k + 1, :] + rate * stat[:, 0:OWN]
    line_steps(steps + FAR_SKEW)

    @pl.loop(0, steps)
    def _(q):
        far = total_of(q, 1 - h)
        remote(far, far, fd_send.at[q], fd_recv.at[q], core).wait_recv()

    @pl.loop(0, steps)
    def _(q):
        inward(q).wait_send()
        across(q).wait_send()

        @pl.when(jnp.logical_not(is_end))
        def _():
            outward(q).wait_send()

    if spread:

        @pl.loop(0, TAPS)
        def _(t):
            far = dw2_ref.at[1 - h, t]
            remote(far, far, ft_send.at[t], ft_recv.at[t], core).wait_recv()
            across_tap(t).wait_send()

        for s in (b, *sources):
            hand_on(gat_of, s, za_send, za_recv, wait_sent)
            hand_on(gtz_of, s, gz_send, gz_recv, wait_sent)
    drain()


def finish_kernel(
    dw1, dw2, out, din, ng, rs, out_to, din_to, dw1_to, dw2_to, ng_to, rs_to, wide, big_sem, small_sem
):
    small = [
        pltpu.make_async_copy(src, dst, small_sem.at[k])
        for k, (src, dst) in enumerate(((out, out_to), (din, din_to), (ng, ng_to), (rs, rs_to)))
    ]
    for copy in small:
        copy.start()

    def write(k, t, half):
        to = (dw1_to, dw2_to)[k]
        return pltpu.make_async_copy(wide.at[k, t, half], to.at[t, pl.ds(HALF * half, HALF)], big_sem.at[k, t, half])

    for k in range(2):

        @pl.loop(0, TAPS)
        def _(t, k=k):
            for half in range(2):
                wide[k, t, half] = (dw1, dw2)[k][half, pl.ds(pl.multiple_of(HALF * t, 16), HALF), :].astype(F32)
                write(k, t, half).start()

    for k in range(2):

        @pl.loop(0, TAPS)
        def _(t, k=k):
            for half in range(2):
                write(k, t, half).wait()

    for copy in small:
        copy.wait()


def shards(features, gains, biases, conv_one, conv_two, out_grad, counts, running_prior, momentum):
    nb = lax.axis_size("batch")
    group = 2 * nb
    spread = nb in SPREAD
    along = 1 if spread else 2
    steps = along * FLAT // STEP
    sources = nb if spread else 1
    hbm = pl.BlockSpec(memory_space=pltpu.HBM)
    in_vmem = pl.BlockSpec(memory_space=pltpu.VMEM)
    dma = pltpu.SemaphoreType.DMA
    vmem = pltpu.VMEM
    maps_out = jax.ShapeDtypeStruct((PIX, OWN), BF16)
    rows_out = jax.ShapeDtypeStruct((4, OWN), F32)
    out, din, dw, dw2, ng, rs = pl.pallas_call(
        functools.partial(block_kernel, nb),
        out_shape=(
            vmem((PIX, OWN), BF16),
            vmem((PIX, OWN), BF16),
            vmem((2, steps, STEP, FULL), BF16),
            vmem((2, TAPS, HALF, FULL) if spread else (8, LANES), BF16 if spread else F32),
            vmem((4, OWN), F32),
            vmem((4, OWN), F32),
        ),
        in_specs=[hbm] * 9,
        out_specs=(in_vmem,) * 6,
        scratch_shapes=[
            vmem((PIX, OWN), BF16),
            vmem((PIX, OWN), BF16),
            vmem((2, OWN), F32),
            vmem((2, OWN), F32),
            vmem((4, OWN), F32),
            pltpu.SMEM((nb,), jnp.int32),
            pltpu.SMEM((1,), F32),
            vmem((TAPS, OWN, FULL), BF16),
            vmem((TAPS, OWN, FULL), BF16),
            vmem((PIX, 2 * LANES), F32),
            vmem((PIX, 2 * LANES), F32),
            vmem((PIX, 2 * LANES), F32),
            vmem((PIX, FULL), F32),
            vmem((PIX, 2 * LANES), F32),
            vmem((PIX, 2 * LANES), F32),
            vmem((CHAN, 8, 2 * LANES), F32),
            vmem((CHAN, 8, LANES), F32),
            vmem((ROWS + 2, WIDE, FULL), BF16),
            vmem((ROWS + 2, WIDE, OWN), BF16),
            vmem((ROWS + 2, WIDE, OWN), BF16),
            vmem((OWN, PIX), BF16),
            vmem((sources, OWN, PIX), BF16),
            *[vmem((group, 8, 2 * LANES), F32)] * 4,
            vmem((CHAN, PACK, LANES), BF16),
            vmem((sources, CHAN, PACK, LANES), BF16),
            *[vmem((CHAN, PACK, LANES), BF16)] * 2,
            vmem((2, CHAN, PACK, LANES), BF16),
            vmem((CHAN, PACK, LANES), F32),
            *[vmem((CHUNKS, HALF, FULL), BF16)] * 2,
            vmem((2 * FLAT, FULL), F32),
            vmem((2 * steps, STEP, FULL), BF16),
            vmem((steps, STEP, FULL), BF16),
            dma((9,)),
            dma((4, group)),
            dma((4, group)),
            *[dma((CHAN,))] * 4,
            *[dma((sources, CHAN))] * 2,
            *[dma((2, nb)), dma((nb,))] * 2,
            *[dma((2, CHAN))] * 2,
            *[dma((3 + sources,))] * 2,
            *[dma((CHUNKS,))] * 2,
            dma((steps,)),
            dma((2 * steps,)),
            *[dma((steps,))] * 4,
            *[dma((TAPS,))] * 2,
            vmem((OWN, FULL), F32),
            *[vmem((ROWS + 2, WIDE, FULL), BF16)] * sources,
            *[vmem((TAPS, OWN, FULL), F32)] * (sources // 2),
        ],
        compiler_params=pltpu.CompilerParams(
            collective_id=0, has_side_effects=True, vmem_limit_bytes=55 * 1024 * 1024
        ),
    )(
        features.reshape(PIX, OWN),
        out_grad.reshape(PIX, OWN),
        gains,
        biases,
        running_prior,
        counts,
        momentum,
        jnp.transpose(conv_one, (1, 2, 0, 3)).reshape(TAPS, OWN, FULL),
        jnp.transpose(conv_two, (1, 2, 0, 3)).reshape(TAPS, OWN, FULL),
    )
    if spread:
        dw1 = dw.reshape(2, FLAT, FULL)
        dw2 = dw2.reshape(2, FLAT, FULL)
    else:
        both = dw.reshape(2, 2, FLAT, FULL)
        dw1, dw2 = both[:, 0], both[:, 1]
    filters_out = jax.ShapeDtypeStruct((TAPS, OWN, FULL), F32)
    out, din, first, second, ng, rs = pl.pallas_call(
        finish_kernel,
        out_shape=(maps_out, maps_out, filters_out, filters_out, rows_out, rows_out),
        in_specs=[in_vmem] * 6,
        out_specs=(hbm,) * 6,
        scratch_shapes=[vmem((2, TAPS, 2, HALF, FULL), F32), dma((2, TAPS, 2)), dma((4,))],
        compiler_params=pltpu.CompilerParams(vmem_limit_bytes=32 * 1024 * 1024),
    )(dw1, dw2, out, din, ng, rs)
    maps = (ROWS, COLS, IMG, OWN)

    def filters(taps):
        return jnp.transpose(taps.reshape(3, 3, OWN, FULL), (2, 0, 1, 3))

    return (out.reshape(maps), din.reshape(maps), filters(first), filters(second), ng, rs)


def solution(mesh):
    maps = P("height", None, "batch", "chan")
    rows = P(None, "chan")
    filters = P("chan", None, None, None)
    return jax.shard_map(
        shards,
        mesh=mesh,
        in_specs=(maps, rows, rows, filters, filters, maps, P(), rows, P()),
        out_specs=(maps, maps, filters, filters, rows, rows),
        check_vma=False,
    )
```

```python
import functools

import jax
import jax.numpy as jnp
from jax import lax
from jax.experimental import pallas as pl
from jax.experimental.pallas import tpu as pltpu
from jax.sharding import PartitionSpec as P

MESH = pl.DeviceIdType.MESH
EPSILON = 1e-05
F32 = jnp.float32
BF16 = jnp.bfloat16

CHAN = 4
ROWS = 4
COLS = 8
IMG = 16
LINE = COLS * IMG
PIX = ROWS * LINE
WIDE = LINE + 2 * IMG
OWN = 160
FULL = CHAN * OWN
LANES = 128
TAIL = OWN - LANES
PACK = PIX + LINE
HALF = OWN // 2
TAPS = 9
CHUNKS = 2 * TAPS
FLAT = TAPS * HALF
STEP = 48
THREE = 3 * HALF
SKEW = 3
FAR_SKEW = 6
SPREAD = (2, 4)


def dot(a, b, contract):
    return lax.dot_general(a, b, ((contract), ((), ())), preferred_element_type=F32)


def turn(x, shift):
    shift = shift % LANES
    return x if shift == 0 else pltpu.roll(x, shift, 1)


def lane_ids(rows):
    return lax.broadcasted_iota(jnp.int32, (rows, LANES), 1)


def pack_tails(tails):
    group = lane_ids(LINE) // TAIL
    packed = tails[0]
    for row in range(1, ROWS):
        packed = jnp.where(group == row, turn(tails[row], TAIL * row), packed)
    return packed


def merge_row(main, tail, row):
    lane = lane_ids(LINE)
    one, two, three = turn(main[1], 32), turn(main[2], 64), turn(main[3], 96)

    def moved(k, to):
        return turn(tail[k], to - TAIL * row)

    return [
        main[0],
        jnp.where(lane < 32, moved(0, 0), one),
        jnp.where(lane < 32, one, jnp.where(lane < 64, moved(1, 32), two)),
        jnp.where(lane < 64, two, jnp.where(lane < 96, moved(2, 64), three)),
        jnp.where(lane < 96, three, moved(3, 96)),
    ]


def split_row(pieces):
    lane = lane_ids(LINE)
    p0, p1, p2, p3, p4 = pieces
    mains = [
        p0,
        jnp.where(lane < 96, turn(p1, -32), turn(p2, -32)),
        jnp.where(lane < 64, turn(p2, -64), turn(p3, -64)),
        jnp.where(lane < 32, turn(p3, 32), turn(p4, 32)),
    ]
    tails = [p1, turn(p2, -32), turn(p3, -64), turn(p4, -96)]
    return mains, tails


def pack_block(dst, main, tails):
    for row in range(ROWS):
        dst[LINE * row : LINE * (row + 1), :] = main(row).astype(dst.dtype)
    dst[PIX:PACK, :] = pack_tails([tails(row) for row in range(ROWS)]).astype(dst.dtype)


def block_kernel(
    nb,
    x_hbm, dy_hbm, gains_hbm, biases_hbm, prior_hbm, counts_hbm, rate_hbm, w1_hbm, w2_hbm,
    out_ref, din_ref, dw_ref, dw2_ref, ng_ref, rs_ref,
    x_ref, dy_ref, gains_ref, biases_ref, prior_ref, counts_ref, rate_ref, w1, w2,
    xf, mid, acc, wide_acc, gact, gpre, prm, prt, a1, g2, gm, gt1, gtz,
    stats0, stats1, stats2, stats3, gx, gat, red0, red1, red_send, own_red,
    d2d_out, d2d_in, part, z_in, z_out,
    ld_sem, st_send, st_recv, pr_send, pr_recv, gx_send, gx_recv, ga_send, ga_recv, za_send, za_recv, gz_send, gz_recv,
    rd_send, rd_recv, ha_send, ha_recv, d2_send, d2_recv, z_send, z_recv, fz_send, fz_recv, fd_send, fd_recv,
    ft_send, ft_recv, product,
    *maps,
):
    b = lax.axis_index("batch")
    h = lax.axis_index("height")
    c = lax.axis_index("chan")
    group = 2 * nb
    me = 2 * b + h
    spread = nb in SPREAD
    home = b if spread else 0
    others = nb - 1 if spread else 0
    along = 1 if spread else 2
    stats, red = (stats0, stats1, stats2, stats3), (red0, red1)
    a2, shares = maps[: others + 1], maps[others + 1 :]

    due, sent = {}, {}

    def drain():
        for f in [*due.values(), *sent.values()]:
            f()

    def arrive(*key):
        due.pop(key)()

    def remote(src, dst, send, recv, to):
        return pltpu.make_async_remote_copy(
            src_ref=src, dst_ref=dst, send_sem=send, recv_sem=recv, device_id=to, device_id_type=MESH
        )

    def over(count, f):
        def run():
            pl.loop(1, count)(f)

        return run

    def at_group(j):
        return (lax.div(j, 2), lax.rem(j, 2), c)

    def at_chan(k):
        return (b, h, k)

    core = (b, 1 - h, c)

    def load(k, src, dst):
        copy = pltpu.make_async_copy(src, dst, ld_sem.at[k])
        copy.start()
        due["load", k] = copy.wait

    for k, (src, dst) in enumerate(
        (
            (x_hbm, x_ref), (counts_hbm, counts_ref), (dy_hbm, dy_ref), (w2_hbm, w2), (gains_hbm, gains_ref),
            (biases_hbm, biases_ref), (w1_hbm, w1), (prior_hbm, prior_ref), (rate_hbm, rate_ref),
        )
    ):
        load(k, src, dst)

    barrier = pltpu.get_barrier_semaphore()

    @pl.loop(1, group)
    def _(d):
        pl.semaphore_signal(barrier, inc=1, device_id=at_group(lax.rem(me + d, group)), device_id_type=MESH)

    @pl.loop(1, CHAN)
    def _(d):
        pl.semaphore_signal(barrier, inc=1, device_id=at_chan(lax.rem(c + d, CHAN)), device_id_type=MESH)

    def line(row):
        return pl.ds(LINE * row, LINE)

    def column_sum(v):
        return jnp.sum(v, axis=0, keepdims=True)

    def stats_copy(e, d):
        j = lax.rem(me + d, group)
        return remote(stats[e].at[j], stats[e].at[j], st_send.at[e, d], st_recv.at[e, j], at_group(j))

    def share_stats(e, first, second):
        keep_stats(e, first, second)
        send_stats(e)

    def keep_stats(e, first, second):
        stats[e][me, 0:1, :] = first
        stats[e][me, 1:2, :] = second

    def send_stats(e):
        @pl.loop(1, group)
        def _(d):
            remote(
                stats[e].at[me], stats[e].at[me], st_send.at[e, d], st_recv.at[e, me],
                at_group(lax.rem(me + d, group)),
            ).start()

        sent["stats", e] = over(group, lambda d: stats_copy(e, d).wait_send())
        due["stats", e] = over(group, lambda d: stats_copy(e, d).wait_recv())

    def sum_stats(e):
        return lax.fori_loop(0, group, lambda j, s: s + stats[e][j], jnp.zeros((8, 2 * LANES), F32))

    def local_stats(src, e):
        here = jnp.full((1, 2 * LANES), count * (ROWS * COLS), jnp.int32).astype(F32)
        s = jnp.zeros((1, 2 * LANES), F32)
        for row in range(ROWS):
            s += column_sum(valid * src[line(row), :])
        mean = s / here
        m2 = jnp.zeros((1, 2 * LANES), F32)
        for row in range(ROWS):
            d = src[line(row), :] - mean
            m2 += column_sum(valid * d * d)
        keep_stats(e, s, m2)

    def norm_stats(e):
        tot = sum_stats(e)
        mean = tot[0:1] / total_row

        def scatter(j, s):
            n = jnp.full((1, 2 * LANES), counts_ref[lax.div(j, 2)] * (ROWS * COLS), jnp.int32).astype(F32)
            d = stats[e][j][0:1] / n - mean
            return s + n * d * d

        var = (tot[1:2] + lax.fori_loop(0, group, scatter, jnp.zeros((1, 2 * LANES), F32))) / total_row
        return mean, var

    def sharing(key, block_of, slot, buf, send, recv):
        def copy(d):
            k = lax.rem(c + d, CHAN)
            return remote(block_of(k), slot, send.at[d], recv.at[c], at_chan(k))

        def taken(d):
            k = lax.rem(c + d, CHAN)
            remote(buf(k), buf(k), send.at[d], recv.at[k], at_chan(k)).wait_recv()

        sent[key] = over(CHAN, lambda d: copy(d).wait_send())
        due[key] = over(CHAN, taken)
        return over(CHAN, lambda d: copy(d).start())

    def share(*how):
        sharing(*how)()

    def hand_on(buf, s, send, recv, act):
        for way, to, ok in ((0, b + 1, (s <= b) & (b + 1 < nb)), (1, b - 1, (s >= b) & (b >= 1))):

            @pl.when(ok)
            def _(way=way, to=to):
                act(remote(buf(s), buf(s), send.at[way, s], recv.at[s], (to, h, c)))

    def start(copy):
        copy.start()

    def wait_sent(copy):
        copy.wait_send()

    def from_batch(buf, s, send, recv):
        remote(buf(s), buf(s), send.at[0, s], recv.at[s], (s, h, c)).wait_recv()

    def share_edge(e, buf):
        copy = remote(buf.at[ROWS - (ROWS - 1) * h], buf.at[(ROWS + 1) * h], ha_send.at[e], ha_recv.at[e], core)
        copy.start()
        sent["edge", e] = copy.wait_send
        far = buf.at[(ROWS + 1) * (1 - h)]
        due["edge", e] = remote(far, far, ha_send.at[e], ha_recv.at[e], core).wait_recv

    def clear_borders(buf):
        lanes = buf.shape[2]
        for row in range(1, ROWS + 1):
            buf[row, 0:IMG, :] = jnp.zeros((IMG, lanes), BF16)
            buf[row, IMG + LINE : WIDE, :] = jnp.zeros((IMG, lanes), BF16)
        buf[(ROWS + 1) * h] = jnp.zeros((WIDE, lanes), BF16)

    def window(buf, i, j):
        return buf[pl.ds(i, ROWS), pl.ds(pl.multiple_of(IMG * j, IMG), LINE), :].reshape(PIX, buf.shape[2])

    def conv_taps(i, src, weights):
        @pl.loop(0, 3)
        def _(j):
            acc[:, 0:OWN] += dot(window(src, i, j), weights[3 * i + j], ((1,), (1,)))

    def conv(src, weights, edge):
        acc[...] = jnp.zeros_like(acc)
        conv_taps(1, src, weights)
        if edge is not None:
            arrive("edge", edge)
        conv_taps(0, src, weights)
        conv_taps(2, src, weights)

    def conv_back_taps(i, src, weights):
        @pl.loop(0, 3)
        def _(j):
            wide_acc[...] += dot(window(src, 2 - i, 2 - j), weights[3 * i + j], ((1,), (0,)))

    def conv_back(src, weights, edge, r):
        wide_acc[...] = jnp.zeros_like(wide_acc)
        conv_back_taps(1, src, weights)
        arrive("edge", edge)
        conv_back_taps(0, src, weights)
        conv_back_taps(2, src, weights)
        back_split(r)

    def back_split(r):
        tails = [[], [], [], []]
        for row in range(ROWS):
            pieces = [wide_acc[line(row), LANES * t : LANES * (t + 1)] for t in range(5)]
            mains, ends = split_row(pieces)
            for k in range(CHAN):
                own_red[k, line(row), :] = mains[k]
                tails[k].append(ends[k])
        for k in range(CHAN):
            own_red[k, PIX:PACK, :] = pack_tails(tails[k])

        @pl.loop(0, CHAN)
        def _(k):
            red_send[r, k] = own_red[k].astype(BF16)

    def share_sums(r):
        share(
            ("red", r), lambda k: red_send.at[r, k], red[r].at[c], lambda k: red[r].at[k], rd_send.at[r], rd_recv.at[r]
        )

    def gather_sum(r):
        arrive("red", r)

        def add(d, s):
            return s + red[r][lax.rem(c + d, CHAN)].astype(F32)

        packed = lax.fori_loop(1, CHAN, add, own_red[c])
        lane = lane_ids(LINE)
        tail = packed[PIX:PACK]
        for row in range(ROWS):
            gact[line(row), 0:LANES] = packed[LINE * row : LINE * (row + 1)]
            gact[line(row), LANES : 2 * LANES] = jnp.where(lane < TAIL, turn(tail, -TAIL * row), 0.0)

    def back_sums(src, mean, inv, gain, bias, e):
        s_gain = jnp.zeros((1, 2 * LANES), F32)
        s_bias = jnp.zeros((1, 2 * LANES), F32)
        for row in range(ROWS):
            hat = (src[line(row), :] - mean) * inv
            pre = gain * hat + bias
            sig = jax.nn.sigmoid(pre)
            grad = gact[line(row), :] * (sig * (1.0 + pre * (1.0 - sig)))
            gpre[line(row), :] = grad
            s_gain += column_sum(valid * grad * hat)
            s_bias += column_sum(valid * grad)
        share_stats(e, s_gain, s_bias)

    def norm_back(src, mean, inv, scale, sums, row):
        hat = (src[line(row), :] - mean) * inv
        return valid * scale * (gpre[line(row), :] - sums[1:2] / total_row - hat * (sums[0:1] / total_row))

    def place(dst, row, pieces):
        for t, piece in enumerate(pieces):
            dst[1 + row, IMG : IMG + LINE, LANES * t : LANES * (t + 1)] = piece.astype(BF16)

    def filter_turn(src, dst):
        for row in range(ROWS):
            flipped = src[1 + row, IMG : IMG + LINE, :].astype(F32).T
            gpre[0:OWN, 0:LANES] = flipped
            dst[0:HALF, line(row)] = gpre[pl.ds(pl.multiple_of(HALF * h, 16), HALF), 0:LANES].astype(BF16)
            dst[HALF:OWN, line(row)] = gpre[pl.ds(pl.multiple_of(HALF * (1 - h), 16), HALF), 0:LANES].astype(BF16)

    def tap_rows(k, t):
        return pl.ds(pl.multiple_of(FLAT * k + HALF * t, 16), HALF)

    def halves(k, t):
        at = TAPS * k + t
        return remote(d2d_out.at[at], d2d_in.at[at], d2_send.at[at], d2_recv.at[at], core)

    def give(k, t, r):
        at = tap_rows(k, t)
        part[at, :] = r[0:HALF]
        d2d_out[TAPS * k + t] = r[HALF:OWN].astype(BF16)
        halves(k, t).start()

    def taps_of(turned, src, first, last, take):
        for i in range(first // 3, last // 3):

            @pl.loop(0, 3)
            def _(j, i=i):
                take(3 * i + j, dot(turned(), window(src, i, j), ((1,), (0,))))

    def halves_sent(k):
        def done():
            @pl.loop(0, TAPS)
            def _(t):
                halves(k, t).wait_send()

        sent["halves", k] = done

    middle = nb // 2
    left = b < middle
    is_end = jnp.logical_or(b == 0, b == nb - 1)
    is_mid = jnp.logical_or(b == middle - 1, b == middle)
    inner = (jnp.where(left, b + 1, b - 1), h, c)
    outer = (jnp.where(left, b - 1, b + 1), h, c)
    steps = along * FLAT // STEP
    mid_off = jnp.where(is_mid, steps, 0)

    def rows_of(q):
        return pl.ds(pl.multiple_of(STEP * q, 16), STEP)

    def inward(q):
        return remote(z_out.at[q], z_in.at[q + mid_off], z_send.at[q], z_recv.at[q + mid_off], inner)

    def total_of(q, half):
        return dw_ref.at[half, q]

    def outward(q):
        return remote(total_of(q, h), total_of(q, h), fz_send.at[q], fz_recv.at[q], outer)

    def across(q):
        return remote(total_of(q, h), total_of(q, h), fd_send.at[q], fd_recv.at[q], core)

    def across_tap(t):
        return remote(dw2_ref.at[h, t], dw2_ref.at[h, t], ft_send.at[t], ft_recv.at[t], core)

    def take_halves(k, g):
        for t in range(3 * g, 3 * g + 3):
            halves(k, t).wait_recv()
            at = tap_rows(k, t)
            part[at, :] = part[at, :] + d2d_in[TAPS * k + t].astype(F32)

        @pl.when(is_end)
        def _():
            first = k * (FLAT // STEP) + 5 * g
            for q in range(first, first + 5):
                z_out[q] = part[rows_of(q), :].astype(BF16)
                inward(q).start()

    def take_final(first, last):
        @pl.loop(first, last)
        def _(t):
            halves(1, t).wait_recv()
            at = tap_rows(1, t)
            dw2_ref[h, t] = (part[at, :] + d2d_in[TAPS + t].astype(F32)).astype(BF16)
            across_tap(t).start()

    def line_step(t):
        @pl.when(jnp.logical_and(t < steps, jnp.logical_not(is_end)))
        def _():
            remote(z_in.at[t], z_in.at[t], z_send.at[t], z_recv.at[t], outer).wait_recv()
            z_out[t] = (part[rows_of(t), :] + z_in[t].astype(F32)).astype(BF16)
            inward(t).start()

        u = t - SKEW

        @pl.when(jnp.logical_and(is_mid, jnp.logical_and(u >= 0, u < steps)))
        def _():
            met = steps + u
            remote(z_in.at[met], z_in.at[met], z_send.at[u], z_recv.at[met], inner).wait_recv()
            dw_ref[h, u] = (z_out[u].astype(F32) + z_in[met].astype(F32)).astype(BF16)

            @pl.when(jnp.logical_not(is_end))
            def _():
                outward(u).start()

            across(u).start()

        v = t - FAR_SKEW

        @pl.when(jnp.logical_and(jnp.logical_not(is_mid), jnp.logical_and(v >= 0, v < steps)))
        def _():
            remote(total_of(v, h), total_of(v, h), fz_send.at[v], fz_recv.at[v], inner).wait_recv()

            @pl.when(jnp.logical_not(is_end))
            def _():
                outward(v).start()

            across(v).start()

    steps_done = [0]

    def line_steps(count):
        first = steps_done[0]
        last = min(first + count, steps + FAR_SKEW)
        if last > first:
            pl.loop(first, last)(line_step)
        steps_done[0] = last

    flip = lax.div(b, max(middle, 1))
    from_end = b + flip * (nb - 1 - 2 * b)

    def source(i):
        s = i + lax.div(i + nb - from_end, nb)
        return s + flip * (nb - 1 - 2 * s)

    sources = [source(i) for i in range(others)]

    def gat_of(s):
        return gat.at[s, c]

    def gtz_of(s):
        return gtz.at[s]

    def share_act(i, s):
        return sharing(
            ("act", i), lambda k: gat.at[s, c], gat.at[s, c], lambda k: gat.at[s, k], ga_send.at[s], ga_recv.at[s]
        )

    def pass_on(first, last):
        for i in range(first, min(last, others)):
            s = sources[i]
            from_batch(gat_of, s, za_send, za_recv)
            hand_on(gat_of, s, za_send, za_recv, start)
            share_act(1 + i, s)()

    def pass_turned(first, last):
        for i in range(first, min(last, others)):
            from_batch(gtz_of, sources[i], gz_send, gz_recv)
            hand_on(gtz_of, sources[i], gz_send, gz_recv, start)

    def inside(f, *a):
        pl.when(jnp.logical_not(is_end))(lambda: f(*a))

    def outside(f, *a):
        pl.when(is_end)(lambda: f(*a))

    def spread_out(i):
        s = home if i == 0 else sources[i - 1]
        arrive("act", i)
        tails = [gat[s, k, PIX:PACK, :].astype(F32) for k in range(CHAN)]
        for row in range(ROWS):
            place(a2[i], row, merge_row([gat[s, k, line(row), :].astype(F32) for k in range(CHAN)], tails, row))
        share_edge(3 + i, a2[i])

    def second_grad(i, first, last):
        s = home if i == 0 else sources[i - 1]
        def take(t, r):
            if not spread:
                give(1, t, r)
            elif i % 2 == 0:
                shares[i // 2][t] = r
            else:
                product[...] = r
                both = shares[i // 2][t] + product[...]
                if i < others:
                    shares[i // 2][t] = both
                elif i == 1:
                    give(1, t, both)
                else:
                    give(1, t, shares[0][t] + both)

        taps_of(lambda: gtz[s], a2[i], first, last, take)

    for buf in (g2, a1, gm, *a2):
        clear_borders(buf)
    prm[c] = jnp.zeros((8, 2 * LANES), F32)
    arrive("load", 0)
    xf[:, LANES : 2 * LANES] = jnp.zeros((PIX, LANES), F32)
    xf[:, 0:OWN] = x_ref[...].astype(F32)
    pack_block(gx.at[c], lambda row: xf[line(row), 0:LANES], lambda row: xf[line(row), LANES : 2 * LANES])

    arrive("load", 1)
    count = counts_ref[b]
    valid = (lax.broadcasted_iota(jnp.int32, (LINE, 2 * LANES), 0) % IMG < count).astype(F32)
    total_images = lax.fori_loop(0, nb, lambda i, s: s + counts_ref[i], jnp.int32(0))
    total_row = jnp.full((1, 2 * LANES), total_images * (COLS * COLS), jnp.int32).astype(F32)

    arrive("load", 2)
    for row in range(ROWS):
        g2[1 + row, IMG : IMG + LINE, :] = (dy_ref[line(row), :].astype(F32) * valid[:, 0:OWN]).astype(BF16)

    local_stats(xf, 0)
    pl.semaphore_wait(barrier, group - 1 + CHAN - 1)
    share(("gx",), lambda k: gx.at[c], gx.at[c], lambda k: gx.at[k], gx_send, gx_recv)
    send_stats(0)
    share_edge(0, g2)

    arrive("load", 4)
    arrive("load", 5)
    prm[c, 2:3, 0:OWN] = gains_ref[0:1, :]
    prm[c, 3:4, 0:OWN] = biases_ref[0:1, :]
    prm[c, 4:5, 0:OWN] = gains_ref[1:2, :]
    prm[c, 5:6, 0:OWN] = biases_ref[1:2, :]
    gain1, bias1, gain2, bias2 = (prm[c, k : k + 1, :] for k in range(2, 6))

    filter_turn(g2, gtz.at[home])
    arrive("stats", 0)
    mean1, var1 = norm_stats(0)
    inv1 = lax.rsqrt(var1 + EPSILON)
    prm[c, 0:1, :] = mean1
    prm[c, 1:2, :] = inv1
    share(("prm",), lambda k: prm.at[c], prm.at[c], lambda k: prm.at[k], pr_send, pr_recv)
    if spread:
        hand_on(gtz_of, b, gz_send, gz_recv, start)

    arrive("load", 3)
    conv_back(g2, w2, 0, 0)
    share_sums(0)
    arrive("prm")
    arrive("gx")

    lane8 = lane_ids(8)
    for k in range(CHAN):
        rows = prm[k, :, LANES : 2 * LANES]
        rows = jnp.where(lane8 < TAIL, rows, 0.0)
        prt[k] = rows + turn(rows, TAIL) + turn(rows, 2 * TAIL) + turn(rows, 3 * TAIL)

    def activated(k, at, rows):
        m, i, g, o = (rows[k, r : r + 1, 0:LANES] for r in range(4))
        pre = g * ((gx[k, at, :].astype(F32) - m) * i) + o
        return pre * jax.nn.sigmoid(pre)

    tails = [activated(k, pl.ds(PIX, LINE), prt) for k in range(CHAN)]
    for row in range(ROWS):
        place(a1, row, merge_row([activated(k, line(row), prm) for k in range(CHAN)], tails, row))
    share_edge(1, a1)
    if spread:
        inside(pass_turned, 0, 2)
    arrive("load", 6)
    conv(a1, w1, 1)
    mid[...] = acc[...]

    local_stats(mid, 1)
    send_stats(1)
    arrive("stats", 1)
    mean2, var2 = norm_stats(1)
    inv2 = lax.rsqrt(var2 + EPSILON)
    def activation(row):
        pre = gain2 * ((mid[line(row), :] - mean2) * inv2) + bias2
        return pre * jax.nn.sigmoid(pre)

    acts = [activation(row) for row in range(ROWS)]
    pack_block(gat.at[home, c], lambda row: acts[row][:, 0:LANES], lambda row: acts[row][:, LANES : 2 * LANES])
    share_act(0, home)()
    gather_sum(0)
    back_sums(mid, mean2, inv2, gain2, bias2, 2)
    if spread:
        hand_on(gat_of, b, za_send, za_recv, start)
        inside(pass_turned, 2, others)
    arrive("stats", 2)
    sums2 = sum_stats(2)

    for row in range(ROWS):
        grad = norm_back(mid, mean2, inv2, gain2 * inv2, sums2, row)
        gm[1 + row, IMG : IMG + LINE, :] = grad[:, 0:OWN].astype(BF16)
    share_edge(2, gm)
    filter_turn(gm, gt1)

    def first_grad(g):
        taps_of(lambda: gt1[...], a1, 3 * g, 3 * g + 3, lambda t, r: give(0, t, r))

    first_grad(0)
    first_grad(1)
    take_halves(0, 0)
    pass_on(0, 1)
    inside(pass_on, 1, 2)
    first_grad(2)
    take_halves(0, 1)
    halves_sent(0)
    take_halves(0, 2)
    for i in range(1, others):
        share_act(1 + i, sources[i])

    def work():
        wide_acc[...] = jnp.zeros_like(wide_acc)
        conv_back_taps(1, gm, w1)
        arrive("edge", 2)
        conv_back_taps(0, gm, w1)
        yield 1
        conv_back_taps(2, gm, w1)
        back_split(1)
        share_sums(1)
        yield 1
        outside(pass_on, 1, 2)
        inside(pass_on, 2, others)
        spread_out(0)
        if spread:
            outside(pass_turned, 0, others)
        yield 1
        for n, g in enumerate((1, 0, 2)):
            if n == 1:
                arrive("edge", 3)
            second_grad(0, 3 * g, 3 * g + 3)
            yield 1
        if not spread:
            halves_sent(1)
            for g in range(3):
                take_halves(1, g)
        outside(pass_on, 2, others)
        acc[...] = jnp.zeros_like(acc)
        for i in range(3):
            conv_taps(i, a2[0], w2)
            yield 1
        for row in range(ROWS):
            kept = (xf[line(row), :] + acc[line(row), :]) * valid
            out_ref[line(row), :] = kept[:, 0:OWN].astype(BF16)
        for i in range(1, others + 1):
            spread_out(i)
            yield 1
            if i == min(2, others):
                gather_sum(1)
                back_sums(xf, mean1, inv1, gain1, bias1, 3)
                yield 1
            for n, g in enumerate((1, 0, 2)):
                if n == 1:
                    arrive("edge", 3 + i)
                second_grad(i, 3 * g, 3 * g + 3)
                if i == others and n > 0:
                    last = (1, 0)[n - 1]
                    take_final(3 * last, 3 * last + 3)
                yield 1
        if not spread:
            gather_sum(1)
            back_sums(xf, mean1, inv1, gain1, bias1, 3)
        if spread:
            halves_sent(1)
            take_final(6, TAPS)
        yield 1

    for count in work():
        line_steps(count)

    arrive("stats", 3)
    sums1 = sum_stats(3)
    for row in range(ROWS):
        grad = norm_back(xf, mean1, inv1, gain1 * inv1, sums1, row)
        din_ref[line(row), :] = (dy_ref[line(row), :].astype(F32) * valid[:, 0:OWN] + grad[:, 0:OWN]).astype(BF16)
    ng_ref[0:2, :] = sums1[0:2, 0:OWN]
    ng_ref[2:4, :] = sums2[0:2, 0:OWN]
    arrive("load", 7)
    arrive("load", 8)
    unbias = total_row / (total_row - 1.0)
    rate = rate_ref[0]
    for k, stat in enumerate((mean1, var1 * unbias, mean2, var2 * unbias)):
        rs_ref[k : k + 1, :] = (1.0 - rate) * prior_ref[k : k + 1, :] + rate * stat[:, 0:OWN]
    line_steps(steps + FAR_SKEW)

    @pl.loop(0, steps)
    def _(q):
        far = total_of(q, 1 - h)
        remote(far, far, fd_send.at[q], fd_recv.at[q], core).wait_recv()

    @pl.loop(0, steps)
    def _(q):
        inward(q).wait_send()
        across(q).wait_send()

        @pl.when(jnp.logical_not(is_end))
        def _():
            outward(q).wait_send()

    if spread:

        @pl.loop(0, TAPS)
        def _(t):
            far = dw2_ref.at[1 - h, t]
            remote(far, far, ft_send.at[t], ft_recv.at[t], core).wait_recv()
            across_tap(t).wait_send()

        for s in (b, *sources):
            hand_on(gat_of, s, za_send, za_recv, wait_sent)
            hand_on(gtz_of, s, gz_send, gz_recv, wait_sent)
    drain()


def finish_kernel(
    dw1, dw2, out, din, ng, rs, out_to, din_to, dw1_to, dw2_to, ng_to, rs_to, wide, big_sem, small_sem
):
    small = [
        pltpu.make_async_copy(src, dst, small_sem.at[k])
        for k, (src, dst) in enumerate(((out, out_to), (din, din_to), (ng, ng_to), (rs, rs_to)))
    ]
    for copy in small:
        copy.start()

    def write(k, t, half):
        to = (dw1_to, dw2_to)[k]
        return pltpu.make_async_copy(wide.at[k, t, half], to.at[t, pl.ds(HALF * half, HALF)], big_sem.at[k, t, half])

    for k in range(2):

        @pl.loop(0, TAPS)
        def _(t, k=k):
            for half in range(2):
                wide[k, t, half] = (dw1, dw2)[k][half, pl.ds(pl.multiple_of(HALF * t, 16), HALF), :].astype(F32)
                write(k, t, half).start()

    for k in range(2):

        @pl.loop(0, TAPS)
        def _(t, k=k):
            for half in range(2):
                write(k, t, half).wait()

    for copy in small:
        copy.wait()


def shards(features, gains, biases, conv_one, conv_two, out_grad, counts, running_prior, momentum):
    nb = lax.axis_size("batch")
    group = 2 * nb
    spread = nb in SPREAD
    along = 1 if spread else 2
    steps = along * FLAT // STEP
    sources = nb if spread else 1
    hbm = pl.BlockSpec(memory_space=pltpu.HBM)
    in_vmem = pl.BlockSpec(memory_space=pltpu.VMEM)
    dma = pltpu.SemaphoreType.DMA
    vmem = pltpu.VMEM
    maps_out = jax.ShapeDtypeStruct((PIX, OWN), BF16)
    rows_out = jax.ShapeDtypeStruct((4, OWN), F32)
    out, din, dw, dw2, ng, rs = pl.pallas_call(
        functools.partial(block_kernel, nb),
        out_shape=(
            vmem((PIX, OWN), BF16),
            vmem((PIX, OWN), BF16),
            vmem((2, steps, STEP, FULL), BF16),
            vmem((2, TAPS, HALF, FULL) if spread else (8, LANES), BF16 if spread else F32),
            vmem((4, OWN), F32),
            vmem((4, OWN), F32),
        ),
        in_specs=[hbm] * 9,
        out_specs=(in_vmem,) * 6,
        scratch_shapes=[
            vmem((PIX, OWN), BF16),
            vmem((PIX, OWN), BF16),
            vmem((2, OWN), F32),
            vmem((2, OWN), F32),
            vmem((4, OWN), F32),
            pltpu.SMEM((nb,), jnp.int32),
            pltpu.SMEM((1,), F32),
            vmem((TAPS, OWN, FULL), BF16),
            vmem((TAPS, OWN, FULL), BF16),
            vmem((PIX, 2 * LANES), F32),
            vmem((PIX, 2 * LANES), F32),
            vmem((PIX, 2 * LANES), F32),
            vmem((PIX, FULL), F32),
            vmem((PIX, 2 * LANES), F32),
            vmem((PIX, 2 * LANES), F32),
            vmem((CHAN, 8, 2 * LANES), F32),
            vmem((CHAN, 8, LANES), F32),
            vmem((ROWS + 2, WIDE, FULL), BF16),
            vmem((ROWS + 2, WIDE, OWN), BF16),
            vmem((ROWS + 2, WIDE, OWN), BF16),
            vmem((OWN, PIX), BF16),
            vmem((sources, OWN, PIX), BF16),
            *[vmem((group, 8, 2 * LANES), F32)] * 4,
            vmem((CHAN, PACK, LANES), BF16),
            vmem((sources, CHAN, PACK, LANES), BF16),
            *[vmem((CHAN, PACK, LANES), BF16)] * 2,
            vmem((2, CHAN, PACK, LANES), BF16),
            vmem((CHAN, PACK, LANES), F32),
            *[vmem((CHUNKS, HALF, FULL), BF16)] * 2,
            vmem((2 * FLAT, FULL), F32),
            vmem((2 * steps, STEP, FULL), BF16),
            vmem((steps, STEP, FULL), BF16),
            dma((9,)),
            dma((4, group)),
            dma((4, group)),
            *[dma((CHAN,))] * 4,
            *[dma((sources, CHAN))] * 2,
            *[dma((2, nb)), dma((nb,))] * 2,
            *[dma((2, CHAN))] * 2,
            *[dma((3 + sources,))] * 2,
            *[dma((CHUNKS,))] * 2,
            dma((steps,)),
            dma((2 * steps,)),
            *[dma((steps,))] * 4,
            *[dma((TAPS,))] * 2,
            vmem((OWN, FULL), F32),
            *[vmem((ROWS + 2, WIDE, FULL), BF16)] * sources,
            *[vmem((TAPS, OWN, FULL), F32)] * (sources // 2),
        ],
        compiler_params=pltpu.CompilerParams(
            collective_id=0, has_side_effects=True, vmem_limit_bytes=55 * 1024 * 1024
        ),
    )(
        features.reshape(PIX, OWN),
        out_grad.reshape(PIX, OWN),
        gains,
        biases,
        running_prior,
        counts,
        momentum,
        jnp.transpose(conv_one, (1, 2, 0, 3)).reshape(TAPS, OWN, FULL),
        jnp.transpose(conv_two, (1, 2, 0, 3)).reshape(TAPS, OWN, FULL),
    )
    if spread:
        dw1 = dw.reshape(2, FLAT, FULL)
        dw2 = dw2.reshape(2, FLAT, FULL)
    else:
        both = dw.reshape(2, 2, FLAT, FULL)
        dw1, dw2 = both[:, 0], both[:, 1]
    filters_out = jax.ShapeDtypeStruct((TAPS, OWN, FULL), F32)
    out, din, first, second, ng, rs = pl.pallas_call(
        finish_kernel,
        out_shape=(maps_out, maps_out, filters_out, filters_out, rows_out, rows_out),
        in_specs=[in_vmem] * 6,
        out_specs=(hbm,) * 6,
        scratch_shapes=[vmem((2, TAPS, 2, HALF, FULL), F32), dma((2, TAPS, 2)), dma((4,))],
        compiler_params=pltpu.CompilerParams(vmem_limit_bytes=32 * 1024 * 1024),
    )(dw1, dw2, out, din, ng, rs)
    maps = (ROWS, COLS, IMG, OWN)

    def filters(taps):
        return jnp.transpose(taps.reshape(3, 3, OWN, FULL), (2, 0, 1, 3))

    return (out.reshape(maps), din.reshape(maps), filters(first), filters(second), ng, rs)


def solution(mesh):
    maps = P("height", None, "batch", "chan")
    rows = P(None, "chan")
    filters = P("chan", None, None, None)
    return jax.shard_map(
        shards,
        mesh=mesh,
        in_specs=(maps, rows, rows, filters, filters, maps, P(), rows, P()),
        out_specs=(maps, maps, filters, filters, rows, rows),
        check_vma=False,
    )
```

```python
import functools

import jax
import jax.numpy as jnp
from jax import lax
from jax.experimental import pallas as pl
from jax.experimental.pallas import tpu as pltpu
from jax.sharding import PartitionSpec as P

MESH = pl.DeviceIdType.MESH
EPSILON = 1e-05
F32 = jnp.float32
BF16 = jnp.bfloat16

CHAN = 4
ROWS = 4
COLS = 8
IMG = 16
LINE = COLS * IMG
PIX = ROWS * LINE
WIDE = LINE + 2 * IMG
OWN = 160
FULL = CHAN * OWN
LANES = 128
TAIL = OWN - LANES
PACK = PIX + LINE
HALF = OWN // 2
TAPS = 9
CHUNKS = 2 * TAPS
FLAT = TAPS * HALF
STEP = 48
THREE = 3 * HALF
SKEW = 3
FAR_SKEW = 6
SPREAD = (2, 4)


def dot(a, b, contract):
    return lax.dot_general(a, b, ((contract), ((), ())), preferred_element_type=F32)


def turn(x, shift):
    shift = shift % LANES
    return x if shift == 0 else pltpu.roll(x, shift, 1)


def lane_ids(rows):
    return lax.broadcasted_iota(jnp.int32, (rows, LANES), 1)


def pack_tails(tails):
    group = lane_ids(LINE) // TAIL
    packed = tails[0]
    for row in range(1, ROWS):
        packed = jnp.where(group == row, turn(tails[row], TAIL * row), packed)
    return packed


def merge_row(main, tail, row):
    lane = lane_ids(LINE)
    one, two, three = turn(main[1], 32), turn(main[2], 64), turn(main[3], 96)

    def moved(k, to):
        return turn(tail[k], to - TAIL * row)

    return [
        main[0],
        jnp.where(lane < 32, moved(0, 0), one),
        jnp.where(lane < 32, one, jnp.where(lane < 64, moved(1, 32), two)),
        jnp.where(lane < 64, two, jnp.where(lane < 96, moved(2, 64), three)),
        jnp.where(lane < 96, three, moved(3, 96)),
    ]


def split_row(pieces):
    lane = lane_ids(LINE)
    p0, p1, p2, p3, p4 = pieces
    mains = [
        p0,
        jnp.where(lane < 96, turn(p1, -32), turn(p2, -32)),
        jnp.where(lane < 64, turn(p2, -64), turn(p3, -64)),
        jnp.where(lane < 32, turn(p3, 32), turn(p4, 32)),
    ]
    tails = [p1, turn(p2, -32), turn(p3, -64), turn(p4, -96)]
    return mains, tails


def pack_block(dst, main, tails):
    for row in range(ROWS):
        dst[LINE * row : LINE * (row + 1), :] = main(row).astype(dst.dtype)
    dst[PIX:PACK, :] = pack_tails([tails(row) for row in range(ROWS)]).astype(dst.dtype)


def block_kernel(
    nb,
    x_hbm, dy_hbm, gains_hbm, biases_hbm, prior_hbm, counts_hbm, rate_hbm, w1_hbm, w2_hbm,
    out_ref, din_ref, dw_ref, dw2_ref, ng_ref, rs_ref,
    x_ref, dy_ref, gains_ref, biases_ref, prior_ref, counts_ref, rate_ref, w1, w2,
    xf, mid, acc, wide_acc, gact, gpre, prm, prt, a1, g2, gm, gt1, gtz,
    stats0, stats1, stats2, stats3, gx, gat, red0, red1, red_send, own_red,
    d2d_out, d2d_in, part, z_in, z_out,
    ld_sem, st_send, st_recv, pr_send, pr_recv, gx_send, gx_recv, ga_send, ga_recv, za_send, za_recv, gz_send, gz_recv,
    rd_send, rd_recv, ha_send, ha_recv, d2_send, d2_recv, z_send, z_recv, fz_send, fz_recv, fd_send, fd_recv,
    ft_send, ft_recv, product,
    *maps,
):
    b = lax.axis_index("batch")
    h = lax.axis_index("height")
    c = lax.axis_index("chan")
    group = 2 * nb
    me = 2 * b + h
    spread = nb in SPREAD
    home = b if spread else 0
    others = nb - 1 if spread else 0
    along = 1 if spread else 2
    stats, red = (stats0, stats1, stats2, stats3), (red0, red1)
    a2, shares = maps[: others + 1], maps[others + 1 :]

    due, sent = {}, {}

    def drain():
        for f in [*due.values(), *sent.values()]:
            f()

    def arrive(*key):
        due.pop(key)()

    def remote(src, dst, send, recv, to):
        return pltpu.make_async_remote_copy(
            src_ref=src, dst_ref=dst, send_sem=send, recv_sem=recv, device_id=to, device_id_type=MESH
        )

    def over(count, f):
        def run():
            pl.loop(1, count)(f)

        return run

    def at_group(j):
        return (lax.div(j, 2), lax.rem(j, 2), c)

    def at_chan(k):
        return (b, h, k)

    core = (b, 1 - h, c)

    def load(k, src, dst):
        copy = pltpu.make_async_copy(src, dst, ld_sem.at[k])
        copy.start()
        due["load", k] = copy.wait

    for k, (src, dst) in enumerate(
        (
            (x_hbm, x_ref), (counts_hbm, counts_ref), (dy_hbm, dy_ref), (w2_hbm, w2), (gains_hbm, gains_ref),
            (biases_hbm, biases_ref), (w1_hbm, w1), (prior_hbm, prior_ref), (rate_hbm, rate_ref),
        )
    ):
        load(k, src, dst)

    barrier = pltpu.get_barrier_semaphore()

    @pl.loop(1, group)
    def _(d):
        pl.semaphore_signal(barrier, inc=1, device_id=at_group(lax.rem(me + d, group)), device_id_type=MESH)

    @pl.loop(1, CHAN)
    def _(d):
        pl.semaphore_signal(barrier, inc=1, device_id=at_chan(lax.rem(c + d, CHAN)), device_id_type=MESH)

    def line(row):
        return pl.ds(LINE * row, LINE)

    def column_sum(v):
        return jnp.sum(v, axis=0, keepdims=True)

    def stats_copy(e, d):
        j = lax.rem(me + d, group)
        return remote(stats[e].at[j], stats[e].at[j], st_send.at[e, d], st_recv.at[e, j], at_group(j))

    def share_stats(e, first, second):
        keep_stats(e, first, second)
        send_stats(e)

    def keep_stats(e, first, second):
        stats[e][me, 0:1, :] = first
        stats[e][me, 1:2, :] = second

    def send_stats(e):
        @pl.loop(1, group)
        def _(d):
            remote(
                stats[e].at[me], stats[e].at[me], st_send.at[e, d], st_recv.at[e, me],
                at_group(lax.rem(me + d, group)),
            ).start()

        sent["stats", e] = over(group, lambda d: stats_copy(e, d).wait_send())
        due["stats", e] = over(group, lambda d: stats_copy(e, d).wait_recv())

    def sum_stats(e):
        return lax.fori_loop(0, group, lambda j, s: s + stats[e][j], jnp.zeros((8, 2 * LANES), F32))

    def local_stats(src, e):
        here = jnp.full((1, 2 * LANES), count * (ROWS * COLS), jnp.int32).astype(F32)
        s = jnp.zeros((1, 2 * LANES), F32)
        for row in range(ROWS):
            s += column_sum(valid * src[line(row), :])
        mean = s / here
        m2 = jnp.zeros((1, 2 * LANES), F32)
        for row in range(ROWS):
            d = src[line(row), :] - mean
            m2 += column_sum(valid * d * d)
        keep_stats(e, s, m2)

    def norm_stats(e):
        tot = sum_stats(e)
        mean = tot[0:1] / total_row

        def scatter(j, s):
            n = jnp.full((1, 2 * LANES), counts_ref[lax.div(j, 2)] * (ROWS * COLS), jnp.int32).astype(F32)
            d = stats[e][j][0:1] / n - mean
            return s + n * d * d

        var = (tot[1:2] + lax.fori_loop(0, group, scatter, jnp.zeros((1, 2 * LANES), F32))) / total_row
        return mean, var

    def sharing(key, block_of, slot, buf, send, recv):
        def copy(d):
            k = lax.rem(c + d, CHAN)
            return remote(block_of(k), slot, send.at[d], recv.at[c], at_chan(k))

        def taken(d):
            k = lax.rem(c + d, CHAN)
            remote(buf(k), buf(k), send.at[d], recv.at[k], at_chan(k)).wait_recv()

        sent[key] = over(CHAN, lambda d: copy(d).wait_send())
        due[key] = over(CHAN, taken)
        return over(CHAN, lambda d: copy(d).start())

    def share(*how):
        sharing(*how)()

    def hand_on(buf, s, send, recv, act):
        for way, to, ok in ((0, b + 1, (s <= b) & (b + 1 < nb)), (1, b - 1, (s >= b) & (b >= 1))):

            @pl.when(ok)
            def _(way=way, to=to):
                act(remote(buf(s), buf(s), send.at[way, s], recv.at[s], (to, h, c)))

    def start(copy):
        copy.start()

    def wait_sent(copy):
        copy.wait_send()

    def from_batch(buf, s, send, recv):
        remote(buf(s), buf(s), send.at[0, s], recv.at[s], (s, h, c)).wait_recv()

    def share_edge(e, buf):
        copy = remote(buf.at[ROWS - (ROWS - 1) * h], buf.at[(ROWS + 1) * h], ha_send.at[e], ha_recv.at[e], core)
        copy.start()
        sent["edge", e] = copy.wait_send
        far = buf.at[(ROWS + 1) * (1 - h)]
        due["edge", e] = remote(far, far, ha_send.at[e], ha_recv.at[e], core).wait_recv

    def clear_borders(buf):
        lanes = buf.shape[2]
        for row in range(1, ROWS + 1):
            buf[row, 0:IMG, :] = jnp.zeros((IMG, lanes), BF16)
            buf[row, IMG + LINE : WIDE, :] = jnp.zeros((IMG, lanes), BF16)
        buf[(ROWS + 1) * h] = jnp.zeros((WIDE, lanes), BF16)

    def window(buf, i, j):
        return buf[pl.ds(i, ROWS), pl.ds(pl.multiple_of(IMG * j, IMG), LINE), :].reshape(PIX, buf.shape[2])

    def conv_taps(i, src, weights):
        @pl.loop(0, 3)
        def _(j):
            acc[:, 0:OWN] += dot(window(src, i, j), weights[3 * i + j], ((1,), (1,)))

    def conv(src, weights, edge):
        acc[...] = jnp.zeros_like(acc)
        conv_taps(1, src, weights)
        if edge is not None:
            arrive("edge", edge)
        conv_taps(0, src, weights)
        conv_taps(2, src, weights)

    def conv_back_taps(i, src, weights):
        @pl.loop(0, 3)
        def _(j):
            wide_acc[...] += dot(window(src, 2 - i, 2 - j), weights[3 * i + j], ((1,), (0,)))

    def conv_back(src, weights, edge, r):
        wide_acc[...] = jnp.zeros_like(wide_acc)
        conv_back_taps(1, src, weights)
        arrive("edge", edge)
        conv_back_taps(0, src, weights)
        conv_back_taps(2, src, weights)
        back_split(r)

    def back_split(r):
        tails = [[], [], [], []]
        for row in range(ROWS):
            pieces = [wide_acc[line(row), LANES * t : LANES * (t + 1)] for t in range(5)]
            mains, ends = split_row(pieces)
            for k in range(CHAN):
                own_red[k, line(row), :] = mains[k]
                tails[k].append(ends[k])
        for k in range(CHAN):
            own_red[k, PIX:PACK, :] = pack_tails(tails[k])

        @pl.loop(0, CHAN)
        def _(k):
            red_send[r, k] = own_red[k].astype(BF16)

    def share_sums(r):
        share(
            ("red", r), lambda k: red_send.at[r, k], red[r].at[c], lambda k: red[r].at[k], rd_send.at[r], rd_recv.at[r]
        )

    def gather_sum(r):
        arrive("red", r)

        def add(d, s):
            return s + red[r][lax.rem(c + d, CHAN)].astype(F32)

        packed = lax.fori_loop(1, CHAN, add, own_red[c])
        lane = lane_ids(LINE)
        tail = packed[PIX:PACK]
        for row in range(ROWS):
            gact[line(row), 0:LANES] = packed[LINE * row : LINE * (row + 1)]
            gact[line(row), LANES : 2 * LANES] = jnp.where(lane < TAIL, turn(tail, -TAIL * row), 0.0)

    def back_sums(src, mean, inv, gain, bias, e):
        s_gain = jnp.zeros((1, 2 * LANES), F32)
        s_bias = jnp.zeros((1, 2 * LANES), F32)
        for row in range(ROWS):
            hat = (src[line(row), :] - mean) * inv
            pre = gain * hat + bias
            sig = jax.nn.sigmoid(pre)
            grad = gact[line(row), :] * (sig * (1.0 + pre * (1.0 - sig)))
            gpre[line(row), :] = grad
            s_gain += column_sum(valid * grad * hat)
            s_bias += column_sum(valid * grad)
        share_stats(e, s_gain, s_bias)

    def norm_back(src, mean, inv, scale, sums, row):
        hat = (src[line(row), :] - mean) * inv
        return valid * scale * (gpre[line(row), :] - sums[1:2] / total_row - hat * (sums[0:1] / total_row))

    def place(dst, row, pieces):
        for t, piece in enumerate(pieces):
            dst[1 + row, IMG : IMG + LINE, LANES * t : LANES * (t + 1)] = piece.astype(BF16)

    def filter_turn(src, dst):
        for row in range(ROWS):
            flipped = src[1 + row, IMG : IMG + LINE, :].astype(F32).T
            gpre[0:OWN, 0:LANES] = flipped
            dst[0:HALF, line(row)] = gpre[pl.ds(pl.multiple_of(HALF * h, 16), HALF), 0:LANES].astype(BF16)
            dst[HALF:OWN, line(row)] = gpre[pl.ds(pl.multiple_of(HALF * (1 - h), 16), HALF), 0:LANES].astype(BF16)

    def tap_rows(k, t):
        return pl.ds(pl.multiple_of(FLAT * k + HALF * t, 16), HALF)

    def halves(k, t):
        at = TAPS * k + t
        return remote(d2d_out.at[at], d2d_in.at[at], d2_send.at[at], d2_recv.at[at], core)

    def give(k, t, r):
        at = tap_rows(k, t)
        part[at, :] = r[0:HALF]
        d2d_out[TAPS * k + t] = r[HALF:OWN].astype(BF16)
        halves(k, t).start()

    def taps_of(turned, src, first, last, take):
        for i in range(first // 3, last // 3):

            @pl.loop(0, 3)
            def _(j, i=i):
                take(3 * i + j, dot(turned(), window(src, i, j), ((1,), (0,))))

    def halves_sent(k):
        def done():
            @pl.loop(0, TAPS)
            def _(t):
                halves(k, t).wait_send()

        sent["halves", k] = done

    middle = nb // 2
    left = b < middle
    is_end = jnp.logical_or(b == 0, b == nb - 1)
    is_mid = jnp.logical_or(b == middle - 1, b == middle)
    inner = (jnp.where(left, b + 1, b - 1), h, c)
    outer = (jnp.where(left, b - 1, b + 1), h, c)
    steps = along * FLAT // STEP
    mid_off = jnp.where(is_mid, steps, 0)

    def rows_of(q):
        return pl.ds(pl.multiple_of(STEP * q, 16), STEP)

    def inward(q):
        return remote(z_out.at[q], z_in.at[q + mid_off], z_send.at[q], z_recv.at[q + mid_off], inner)

    def total_of(q, half):
        return dw_ref.at[half, q]

    def outward(q):
        return remote(total_of(q, h), total_of(q, h), fz_send.at[q], fz_recv.at[q], outer)

    def across(q):
        return remote(total_of(q, h), total_of(q, h), fd_send.at[q], fd_recv.at[q], core)

    def across_tap(t):
        return remote(dw2_ref.at[h, t], dw2_ref.at[h, t], ft_send.at[t], ft_recv.at[t], core)

    def take_halves(k, g):
        for t in range(3 * g, 3 * g + 3):
            halves(k, t).wait_recv()
            at = tap_rows(k, t)
            part[at, :] = part[at, :] + d2d_in[TAPS * k + t].astype(F32)

        @pl.when(is_end)
        def _():
            first = k * (FLAT // STEP) + 5 * g
            for q in range(first, first + 5):
                z_out[q] = part[rows_of(q), :].astype(BF16)
                inward(q).start()

    def take_final(first, last):
        @pl.loop(first, last)
        def _(t):
            halves(1, t).wait_recv()
            at = tap_rows(1, t)
            dw2_ref[h, t] = (part[at, :] + d2d_in[TAPS + t].astype(F32)).astype(BF16)
            across_tap(t).start()

    def line_step(t):
        @pl.when(jnp.logical_and(t < steps, jnp.logical_not(is_end)))
        def _():
            remote(z_in.at[t], z_in.at[t], z_send.at[t], z_recv.at[t], outer).wait_recv()
            z_out[t] = (part[rows_of(t), :] + z_in[t].astype(F32)).astype(BF16)
            inward(t).start()

        u = t - SKEW

        @pl.when(jnp.logical_and(is_mid, jnp.logical_and(u >= 0, u < steps)))
        def _():
            met = steps + u
            remote(z_in.at[met], z_in.at[met], z_send.at[u], z_recv.at[met], inner).wait_recv()
            dw_ref[h, u] = (z_out[u].astype(F32) + z_in[met].astype(F32)).astype(BF16)

            @pl.when(jnp.logical_not(is_end))
            def _():
                outward(u).start()

            across(u).start()

        v = t - FAR_SKEW

        @pl.when(jnp.logical_and(jnp.logical_not(is_mid), jnp.logical_and(v >= 0, v < steps)))
        def _():
            remote(total_of(v, h), total_of(v, h), fz_send.at[v], fz_recv.at[v], inner).wait_recv()

            @pl.when(jnp.logical_not(is_end))
            def _():
                outward(v).start()

            across(v).start()

    steps_done = [0]

    def line_steps(count):
        first = steps_done[0]
        last = min(first + count, steps + FAR_SKEW)
        if last > first:
            pl.loop(first, last)(line_step)
        steps_done[0] = last

    flip = lax.div(b, max(middle, 1))
    from_end = b + flip * (nb - 1 - 2 * b)

    def source(i):
        s = i + lax.div(i + nb - from_end, nb)
        return s + flip * (nb - 1 - 2 * s)

    sources = [source(i) for i in range(others)]

    def gat_of(s):
        return gat.at[s, c]

    def gtz_of(s):
        return gtz.at[s]

    def share_act(i, s):
        return sharing(
            ("act", i), lambda k: gat.at[s, c], gat.at[s, c], lambda k: gat.at[s, k], ga_send.at[s], ga_recv.at[s]
        )

    def pass_on(first, last):
        for i in range(first, min(last, others)):
            s = sources[i]
            from_batch(gat_of, s, za_send, za_recv)
            hand_on(gat_of, s, za_send, za_recv, start)
            share_act(1 + i, s)()

    def pass_turned(first, last):
        for i in range(first, min(last, others)):
            from_batch(gtz_of, sources[i], gz_send, gz_recv)
            hand_on(gtz_of, sources[i], gz_send, gz_recv, start)

    def inside(f, *a):
        pl.when(jnp.logical_not(is_end))(lambda: f(*a))

    def outside(f, *a):
        pl.when(is_end)(lambda: f(*a))

    def spread_out(i):
        s = home if i == 0 else sources[i - 1]
        arrive("act", i)
        tails = [gat[s, k, PIX:PACK, :].astype(F32) for k in range(CHAN)]
        for row in range(ROWS):
            place(a2[i], row, merge_row([gat[s, k, line(row), :].astype(F32) for k in range(CHAN)], tails, row))
        share_edge(3 + i, a2[i])

    def second_grad(i, first, last):
        s = home if i == 0 else sources[i - 1]
        def take(t, r):
            if not spread:
                give(1, t, r)
            elif i % 2 == 0:
                shares[i // 2][t] = r
            else:
                product[...] = r
                both = shares[i // 2][t] + product[...]
                if i < others:
                    shares[i // 2][t] = both
                elif i == 1:
                    give(1, t, both)
                else:
                    give(1, t, shares[0][t] + both)

        taps_of(lambda: gtz[s], a2[i], first, last, take)

    clear_borders(g2)
    prm[c] = jnp.zeros((8, 2 * LANES), F32)
    arrive("load", 0)
    xf[:, LANES : 2 * LANES] = jnp.zeros((PIX, LANES), F32)
    xf[:, 0:OWN] = x_ref[...].astype(F32)
    pack_block(gx.at[c], lambda row: xf[line(row), 0:LANES], lambda row: xf[line(row), LANES : 2 * LANES])

    arrive("load", 1)
    count = counts_ref[b]
    valid = (lax.broadcasted_iota(jnp.int32, (LINE, 2 * LANES), 0) % IMG < count).astype(F32)
    total_images = lax.fori_loop(0, nb, lambda i, s: s + counts_ref[i], jnp.int32(0))
    total_row = jnp.full((1, 2 * LANES), total_images * (COLS * COLS), jnp.int32).astype(F32)

    arrive("load", 2)
    for row in range(ROWS):
        g2[1 + row, IMG : IMG + LINE, :] = (dy_ref[line(row), :].astype(F32) * valid[:, 0:OWN]).astype(BF16)

    local_stats(xf, 0)
    pl.semaphore_wait(barrier, group - 1 + CHAN - 1)
    share(("gx",), lambda k: gx.at[c], gx.at[c], lambda k: gx.at[k], gx_send, gx_recv)
    send_stats(0)
    share_edge(0, g2)
    for buf in (a1, gm, *a2):
        clear_borders(buf)

    arrive("load", 4)
    arrive("load", 5)
    prm[c, 2:3, 0:OWN] = gains_ref[0:1, :]
    prm[c, 3:4, 0:OWN] = biases_ref[0:1, :]
    prm[c, 4:5, 0:OWN] = gains_ref[1:2, :]
    prm[c, 5:6, 0:OWN] = biases_ref[1:2, :]
    gain1, bias1, gain2, bias2 = (prm[c, k : k + 1, :] for k in range(2, 6))

    filter_turn(g2, gtz.at[home])
    arrive("stats", 0)
    mean1, var1 = norm_stats(0)
    inv1 = lax.rsqrt(var1 + EPSILON)
    prm[c, 0:1, :] = mean1
    prm[c, 1:2, :] = inv1
    share(("prm",), lambda k: prm.at[c], prm.at[c], lambda k: prm.at[k], pr_send, pr_recv)
    if spread:
        hand_on(gtz_of, b, gz_send, gz_recv, start)

    arrive("load", 3)
    conv_back(g2, w2, 0, 0)
    share_sums(0)
    arrive("prm")
    arrive("gx")

    lane8 = lane_ids(8)
    for k in range(CHAN):
        rows = prm[k, :, LANES : 2 * LANES]
        rows = jnp.where(lane8 < TAIL, rows, 0.0)
        prt[k] = rows + turn(rows, TAIL) + turn(rows, 2 * TAIL) + turn(rows, 3 * TAIL)

    def activated(k, at, rows):
        m, i, g, o = (rows[k, r : r + 1, 0:LANES] for r in range(4))
        pre = g * ((gx[k, at, :].astype(F32) - m) * i) + o
        return pre * jax.nn.sigmoid(pre)

    tails = [activated(k, pl.ds(PIX, LINE), prt) for k in range(CHAN)]
    for row in range(ROWS):
        place(a1, row, merge_row([activated(k, line(row), prm) for k in range(CHAN)], tails, row))
    share_edge(1, a1)
    if spread:
        inside(pass_turned, 0, 2)
    arrive("load", 6)
    conv(a1, w1, 1)
    mid[...] = acc[...]

    local_stats(mid, 1)
    send_stats(1)
    arrive("stats", 1)
    mean2, var2 = norm_stats(1)
    inv2 = lax.rsqrt(var2 + EPSILON)
    def activation(row):
        pre = gain2 * ((mid[line(row), :] - mean2) * inv2) + bias2
        return pre * jax.nn.sigmoid(pre)

    acts = [activation(row) for row in range(ROWS)]
    pack_block(gat.at[home, c], lambda row: acts[row][:, 0:LANES], lambda row: acts[row][:, LANES : 2 * LANES])
    share_act(0, home)()
    gather_sum(0)
    back_sums(mid, mean2, inv2, gain2, bias2, 2)
    if spread:
        hand_on(gat_of, b, za_send, za_recv, start)
        inside(pass_turned, 2, others)
    arrive("stats", 2)
    sums2 = sum_stats(2)

    for row in range(ROWS):
        grad = norm_back(mid, mean2, inv2, gain2 * inv2, sums2, row)
        gm[1 + row, IMG : IMG + LINE, :] = grad[:, 0:OWN].astype(BF16)
    share_edge(2, gm)
    filter_turn(gm, gt1)

    def first_grad(g):
        taps_of(lambda: gt1[...], a1, 3 * g, 3 * g + 3, lambda t, r: give(0, t, r))

    first_grad(0)
    first_grad(1)
    take_halves(0, 0)
    pass_on(0, 1)
    inside(pass_on, 1, 2)
    first_grad(2)
    take_halves(0, 1)
    halves_sent(0)
    take_halves(0, 2)
    for i in range(1, others):
        share_act(1 + i, sources[i])

    def work():
        wide_acc[...] = jnp.zeros_like(wide_acc)
        conv_back_taps(1, gm, w1)
        arrive("edge", 2)
        conv_back_taps(0, gm, w1)
        yield 1
        conv_back_taps(2, gm, w1)
        back_split(1)
        share_sums(1)
        yield 1
        outside(pass_on, 1, 2)
        inside(pass_on, 2, others)
        spread_out(0)
        if spread:
            outside(pass_turned, 0, others)
        yield 1
        for n, g in enumerate((1, 0, 2)):
            if n == 1:
                arrive("edge", 3)
            second_grad(0, 3 * g, 3 * g + 3)
            yield 1
        if not spread:
            halves_sent(1)
            for g in range(3):
                take_halves(1, g)
        outside(pass_on, 2, others)
        acc[...] = jnp.zeros_like(acc)
        for i in range(3):
            conv_taps(i, a2[0], w2)
            yield 1
        for row in range(ROWS):
            kept = (xf[line(row), :] + acc[line(row), :]) * valid
            out_ref[line(row), :] = kept[:, 0:OWN].astype(BF16)
        for i in range(1, others + 1):
            spread_out(i)
            yield 1
            if i == min(2, others):
                gather_sum(1)
                back_sums(xf, mean1, inv1, gain1, bias1, 3)
                yield 1
            for n, g in enumerate((1, 0, 2)):
                if n == 1:
                    arrive("edge", 3 + i)
                second_grad(i, 3 * g, 3 * g + 3)
                if i == others and n > 0:
                    last = (1, 0)[n - 1]
                    take_final(3 * last, 3 * last + 3)
                yield 1
        if not spread:
            gather_sum(1)
            back_sums(xf, mean1, inv1, gain1, bias1, 3)
        if spread:
            halves_sent(1)
            take_final(6, TAPS)
        yield 1

    for count in work():
        line_steps(count)

    arrive("stats", 3)
    sums1 = sum_stats(3)
    for row in range(ROWS):
        grad = norm_back(xf, mean1, inv1, gain1 * inv1, sums1, row)
        din_ref[line(row), :] = (dy_ref[line(row), :].astype(F32) * valid[:, 0:OWN] + grad[:, 0:OWN]).astype(BF16)
    ng_ref[0:2, :] = sums1[0:2, 0:OWN]
    ng_ref[2:4, :] = sums2[0:2, 0:OWN]
    arrive("load", 7)
    arrive("load", 8)
    unbias = total_row / (total_row - 1.0)
    rate = rate_ref[0]
    for k, stat in enumerate((mean1, var1 * unbias, mean2, var2 * unbias)):
        rs_ref[k : k + 1, :] = (1.0 - rate) * prior_ref[k : k + 1, :] + rate * stat[:, 0:OWN]
    line_steps(steps + FAR_SKEW)

    @pl.loop(0, steps)
    def _(q):
        far = total_of(q, 1 - h)
        remote(far, far, fd_send.at[q], fd_recv.at[q], core).wait_recv()

    @pl.loop(0, steps)
    def _(q):
        inward(q).wait_send()
        across(q).wait_send()

        @pl.when(jnp.logical_not(is_end))
        def _():
            outward(q).wait_send()

    if spread:

        @pl.loop(0, TAPS)
        def _(t):
            far = dw2_ref.at[1 - h, t]
            remote(far, far, ft_send.at[t], ft_recv.at[t], core).wait_recv()
            across_tap(t).wait_send()

        for s in (b, *sources):
            hand_on(gat_of, s, za_send, za_recv, wait_sent)
            hand_on(gtz_of, s, gz_send, gz_recv, wait_sent)
    drain()


def finish_kernel(
    dw1, dw2, out, din, ng, rs, out_to, din_to, dw1_to, dw2_to, ng_to, rs_to, wide, big_sem, small_sem
):
    small = [
        pltpu.make_async_copy(src, dst, small_sem.at[k])
        for k, (src, dst) in enumerate(((out, out_to), (din, din_to), (ng, ng_to), (rs, rs_to)))
    ]
    for copy in small:
        copy.start()

    def write(k, t, half):
        to = (dw1_to, dw2_to)[k]
        return pltpu.make_async_copy(wide.at[k, t, half], to.at[t, pl.ds(HALF * half, HALF)], big_sem.at[k, t, half])

    for k in range(2):

        @pl.loop(0, TAPS)
        def _(t, k=k):
            for half in range(2):
                wide[k, t, half] = (dw1, dw2)[k][half, pl.ds(pl.multiple_of(HALF * t, 16), HALF), :].astype(F32)
                write(k, t, half).start()

    for k in range(2):

        @pl.loop(0, TAPS)
        def _(t, k=k):
            for half in range(2):
                write(k, t, half).wait()

    for copy in small:
        copy.wait()


def shards(features, gains, biases, conv_one, conv_two, out_grad, counts, running_prior, momentum):
    nb = lax.axis_size("batch")
    group = 2 * nb
    spread = nb in SPREAD
    along = 1 if spread else 2
    steps = along * FLAT // STEP
    sources = nb if spread else 1
    hbm = pl.BlockSpec(memory_space=pltpu.HBM)
    in_vmem = pl.BlockSpec(memory_space=pltpu.VMEM)
    dma = pltpu.SemaphoreType.DMA
    vmem = pltpu.VMEM
    maps_out = jax.ShapeDtypeStruct((PIX, OWN), BF16)
    rows_out = jax.ShapeDtypeStruct((4, OWN), F32)
    out, din, dw, dw2, ng, rs = pl.pallas_call(
        functools.partial(block_kernel, nb),
        out_shape=(
            vmem((PIX, OWN), BF16),
            vmem((PIX, OWN), BF16),
            vmem((2, steps, STEP, FULL), BF16),
            vmem((2, TAPS, HALF, FULL) if spread else (8, LANES), BF16 if spread else F32),
            vmem((4, OWN), F32),
            vmem((4, OWN), F32),
        ),
        in_specs=[hbm] * 9,
        out_specs=(in_vmem,) * 6,
        scratch_shapes=[
            vmem((PIX, OWN), BF16),
            vmem((PIX, OWN), BF16),
            vmem((2, OWN), F32),
            vmem((2, OWN), F32),
            vmem((4, OWN), F32),
            pltpu.SMEM((nb,), jnp.int32),
            pltpu.SMEM((1,), F32),
            vmem((TAPS, OWN, FULL), BF16),
            vmem((TAPS, OWN, FULL), BF16),
            vmem((PIX, 2 * LANES), F32),
            vmem((PIX, 2 * LANES), F32),
            vmem((PIX, 2 * LANES), F32),
            vmem((PIX, FULL), F32),
            vmem((PIX, 2 * LANES), F32),
            vmem((PIX, 2 * LANES), F32),
            vmem((CHAN, 8, 2 * LANES), F32),
            vmem((CHAN, 8, LANES), F32),
            vmem((ROWS + 2, WIDE, FULL), BF16),
            vmem((ROWS + 2, WIDE, OWN), BF16),
            vmem((ROWS + 2, WIDE, OWN), BF16),
            vmem((OWN, PIX), BF16),
            vmem((sources, OWN, PIX), BF16),
            *[vmem((group, 8, 2 * LANES), F32)] * 4,
            vmem((CHAN, PACK, LANES), BF16),
            vmem((sources, CHAN, PACK, LANES), BF16),
            *[vmem((CHAN, PACK, LANES), BF16)] * 2,
            vmem((2, CHAN, PACK, LANES), BF16),
            vmem((CHAN, PACK, LANES), F32),
            *[vmem((CHUNKS, HALF, FULL), BF16)] * 2,
            vmem((2 * FLAT, FULL), F32),
            vmem((2 * steps, STEP, FULL), BF16),
            vmem((steps, STEP, FULL), BF16),
            dma((9,)),
            dma((4, group)),
            dma((4, group)),
            *[dma((CHAN,))] * 4,
            *[dma((sources, CHAN))] * 2,
            *[dma((2, nb)), dma((nb,))] * 2,
            *[dma((2, CHAN))] * 2,
            *[dma((3 + sources,))] * 2,
            *[dma((CHUNKS,))] * 2,
            dma((steps,)),
            dma((2 * steps,)),
            *[dma((steps,))] * 4,
            *[dma((TAPS,))] * 2,
            vmem((OWN, FULL), F32),
            *[vmem((ROWS + 2, WIDE, FULL), BF16)] * sources,
            *[vmem((TAPS, OWN, FULL), F32)] * (sources // 2),
        ],
        compiler_params=pltpu.CompilerParams(
            collective_id=0, has_side_effects=True, vmem_limit_bytes=55 * 1024 * 1024
        ),
    )(
        features.reshape(PIX, OWN),
        out_grad.reshape(PIX, OWN),
        gains,
        biases,
        running_prior,
        counts,
        momentum,
        jnp.transpose(conv_one, (1, 2, 0, 3)).reshape(TAPS, OWN, FULL),
        jnp.transpose(conv_two, (1, 2, 0, 3)).reshape(TAPS, OWN, FULL),
    )
    if spread:
        dw1 = dw.reshape(2, FLAT, FULL)
        dw2 = dw2.reshape(2, FLAT, FULL)
    else:
        both = dw.reshape(2, 2, FLAT, FULL)
        dw1, dw2 = both[:, 0], both[:, 1]
    filters_out = jax.ShapeDtypeStruct((TAPS, OWN, FULL), F32)
    out, din, first, second, ng, rs = pl.pallas_call(
        finish_kernel,
        out_shape=(maps_out, maps_out, filters_out, filters_out, rows_out, rows_out),
        in_specs=[in_vmem] * 6,
        out_specs=(hbm,) * 6,
        scratch_shapes=[vmem((2, TAPS, 2, HALF, FULL), F32), dma((2, TAPS, 2)), dma((4,))],
        compiler_params=pltpu.CompilerParams(vmem_limit_bytes=32 * 1024 * 1024),
    )(dw1, dw2, out, din, ng, rs)
    maps = (ROWS, COLS, IMG, OWN)

    def filters(taps):
        return jnp.transpose(taps.reshape(3, 3, OWN, FULL), (2, 0, 1, 3))

    return (out.reshape(maps), din.reshape(maps), filters(first), filters(second), ng, rs)


def solution(mesh):
    maps = P("height", None, "batch", "chan")
    rows = P(None, "chan")
    filters = P("chan", None, None, None)
    return jax.shard_map(
        shards,
        mesh=mesh,
        in_specs=(maps, rows, rows, filters, filters, maps, P(), rows, P()),
        out_specs=(maps, maps, filters, filters, rows, rows),
        check_vma=False,
    )
```
